32 devices in a mesh: seq: 16 (over z, y, x), tp: 2 (over core).
Axes of the slice: x: 2, y: 2, z: 4, core: 2. Of those that a mesh axis runs over, the one named last changes fastest.
Arguments:
- hidden_in: bfloat16 [4096, 2048], P('seq')
- token_order: int32 [4096], P('seq'), may hold values from 0 to 4095, as said below
- span_lengths: int32 [4], replicated, may hold values from 1 to 2048, 4096 in all
- placement: int32 [32], replicated, may hold values from 0 to 31, as said below
- norm_in: float32 [2048], replicated, may hold values from 0.1 to 1.9
- q_weight: bfloat16 [2048, 2048], P(None, 'tp')
- k_weight: bfloat16 [2048, 1024], P(None, 'tp')
- v_weight: bfloat16 [2048, 1024], P(None, 'tp'), may hold values from -0.125 to 0.125
- q_gain: float32 [128], replicated
- k_gain: float32 [128], replicated
- o_weight: bfloat16 [2048, 2048], P('tp'), may hold values from -0.125 to 0.125
- norm_mid: float32 [2048], replicated, may hold values from 0.1 to 1.9
- gate_weight: bfloat16 [2048, 3072], P(None, 'tp'), may hold values from -0.125 to 0.125
- up_weight: bfloat16 [2048, 3072], P(None, 'tp'), may hold values from -0.125 to 0.125
- down_weight: bfloat16 [3072, 2048], P('tp'), may hold values from -0.109375 to 0.109375
Outputs:
- hidden_out: bfloat16 [4096, 2048], P('seq', 'tp')
- kv_cache: bfloat16 [32, 128, 2048], P('seq', None, 'tp')
The draws below stay inside these ranges and needn't reach their ends.
Inputs may be any that keep to these rules, and one draw needn't show every extreme that they name: `token_order`: a permutation of all tokens; for each block b of 128 consecutive tokens and each seq index d, rows d * 256 + placement[b] * 8 + j, j < 8, hold tokens of block b. `placement`: a permutation of the blocks. `span_lengths`: sum to 4096.
All inputs are finite; a program needn't handle non-finite values.
Results may differ from the reference program's by a relative error of at most 0.022.
The reference program's roundings to bfloat16 on the way count: a program that leaves them out, or rounds other values in their place, can miss the bound.
Values may be sent and summed in bfloat16 or wider, within the bound.
A program may use at most 128 MiB of HBM per device.

```python
import math
import jax
import jax.numpy as jnp
import numpy as np
from jax import lax

D = 2048
H = 16
KVH = 8
HD = 128
FFW = 3072
BLK = 128
TOKENS = 4096
NBLK = 32
SHARE = 8
REQS = 4
N_SEQ = 16


def shared_placement(key):
    return jax.random.permutation(jax.random.fold_in(key, 11), NBLK).astype(jnp.int32)


def draw_placement(key, part):
    return shared_placement(key)


def one_block(block_key):
    return jax.random.permutation(block_key, BLK)


def draw_token_order(key, part):
    place = shared_placement(key)
    keys = jax.random.split(jax.random.fold_in(key, 23), NBLK)
    inner = jax.vmap(one_block)(keys).astype(jnp.int32)
    tokens = inner + (jnp.arange(NBLK, dtype=jnp.int32) * BLK)[:, None]
    tokens = tokens.reshape(NBLK, N_SEQ, SHARE).transpose(1, 0, 2)
    table = jnp.zeros((N_SEQ, NBLK, SHARE), jnp.int32).at[:, place, :].set(tokens)
    return table.reshape(TOKENS)


def gain_values(key):
    return jnp.exp(jax.random.uniform(key, (HD,), jnp.float32, math.log(0.5), math.log(2.0)))


def draw_q_gain(key, part):
    return gain_values(jax.random.fold_in(key, 31))


def draw_k_gain(key, part):
    return gain_values(jax.random.fold_in(key, 37))


def shared_projections(key):
    base = jax.random.fold_in(key, 41)
    spread = D ** (-0.5)
    q_raw = jnp.clip(jax.random.normal(jax.random.fold_in(base, 1), (D, H * HD), jnp.float32), -4.0, 4.0) * spread
    k_raw = jnp.clip(jax.random.normal(jax.random.fold_in(base, 2), (D, KVH * HD), jnp.float32), -4.0, 4.0) * spread
    return (q_raw, k_raw)


def draw_q_weight(key, part):
    return shared_projections(key)[0].astype(jnp.bfloat16)


def draw_k_weight(key, part):
    return shared_projections(key)[1].astype(jnp.bfloat16)


def draw_hidden_in(key, part):
    noise = jnp.clip(jax.random.normal(jax.random.fold_in(key, 43), (TOKENS, D), jnp.float32), -6.0, 6.0)
    return noise.astype(jnp.bfloat16)


def steps_of(stream_key, dims, cuts, smallest, top_value):
    factor_of, own = 1.0, jax.random.fold_in(stream_key, 6)
    for position, blocks in cuts:
        steps = jnp.exp(jax.random.uniform(jax.random.fold_in(own, position), (blocks,), jnp.float32, smallest / len(cuts), top_value / len(cuts)))
        factor_of = factor_of * jnp.repeat(steps, dims[position] // blocks).reshape([-1 if axis == position else 1 for axis in range(len(dims))])
    return factor_of


def profile(amount, total, limit, slope):
    portions = [(1 << 20) // math.isqrt(rank ** slope) + 1 for rank in range(2, amount + 1)]
    spare, given = total - limit - (amount - 1), [1] * (amount - 1)
    while spare > 0:
        candidates = [i for i in range(amount - 1) if given[i] < limit]
        mass, left = sum([portions[i] for i in candidates]), spare
        for i in candidates:
            addition = min(limit - given[i], max(1, left * portions[i] // mass), spare)
            given[i] = given[i] + addition
            spare = spare - addition
    return np.array([limit] + given)


def uneven_parts(stream_key, number_of, total, limit, skew):
    if number_of == 2:
        one = jax.random.randint(stream_key, (), max(1, total - limit), min(limit, total - 1) + 1)
        return jnp.stack([one, total - one])
    sizes = jnp.asarray(profile(number_of, total, limit, skew), jnp.int32)
    twos = (number_of - 1) // 2
    giver, receiver = sizes[1:1 + 2 * twos:2], sizes[2:2 + 2 * twos:2]
    room = jnp.minimum(giver - 1, limit - receiver)
    moved = jax.random.randint(jax.random.fold_in(stream_key, 1), (twos,), 0, 1 << 20) % (room + 1)
    sizes = sizes.at[1:1 + 2 * twos:2].set(giver - moved).at[2:2 + 2 * twos:2].set(receiver + moved)
    return sizes[jax.random.permutation(jax.random.fold_in(stream_key, 2), number_of)]


def centred(rng, dims, deviation, reach, cuts=(), kind=jnp.bfloat16):
    level = steps_of(rng, dims, cuts, -0.22, 0.18) if cuts else 1.0
    result = jax.random.normal(rng, dims, jnp.float32) * deviation * level
    return jnp.minimum(jnp.maximum(result, -reach), reach).astype(kind)


def setup_inputs(seed: int = 0) -> dict:
    streams_of = jax.random.split(jax.random.key(seed), 16)
    return {
        "hidden_in": draw_hidden_in(jax.random.fold_in(streams_of[15], 71), 0),
        "token_order": draw_token_order(jax.random.fold_in(streams_of[15], 71), 0),
        "span_lengths": uneven_parts(streams_of[2], REQS, TOKENS, TOKENS // 2, 2).astype(jnp.int32),
        "placement": draw_placement(jax.random.fold_in(streams_of[15], 71), 0),
        "norm_in": jnp.clip(1.0 + 0.18 * jax.random.normal(streams_of[4], (D,), jnp.float32), 0.1, 1.9),
        "q_weight": draw_q_weight(jax.random.fold_in(streams_of[15], 71), 0),
        "k_weight": draw_k_weight(jax.random.fold_in(streams_of[15], 71), 0),
        "v_weight": centred(streams_of[7], (D, KVH * HD), D ** -0.5, 0.125, ((1, 2),)),
        "q_gain": draw_q_gain(jax.random.fold_in(streams_of[15], 71), 0),
        "k_gain": draw_k_gain(jax.random.fold_in(streams_of[15], 71), 0),
        "o_weight": centred(streams_of[10], (H * HD, D), (H * HD) ** -0.5, 0.125, ((0, 2),)),
        "norm_mid": jnp.clip(1.0 + 0.18 * jax.random.normal(streams_of[11], (D,), jnp.float32), 0.1, 1.9),
        "gate_weight": centred(streams_of[12], (D, FFW), D ** -0.5, 0.125, ((1, 2),)),
        "up_weight": centred(streams_of[13], (D, FFW), D ** -0.5, 0.125, ((1, 2),)),
        "down_weight": centred(streams_of[14], (FFW, D), FFW ** -0.5, 0.109375, ((0, 2),)),
    }


EPS = 1e-06
THETA = 1000000.0

def rms(values, gain):
    return values * lax.rsqrt(lax.optimization_barrier(jnp.mean(values * values, axis=-1, keepdims=True)) + EPS) * gain

def rotary(values, pos):
    half = values.shape[-1] // 2
    freq = THETA ** (-jnp.arange(half, dtype=jnp.float32) * 2.0 / values.shape[-1])
    angle = pos.astype(jnp.float32)[:, None] * freq[None, :]
    cosine = jnp.cos(angle)[:, None, :]
    sine = jnp.sin(angle)[:, None, :]
    first = values[..., :half]
    second = values[..., half:]
    return jnp.concatenate([first * cosine - second * sine, second * cosine + first * sine], axis=-1)

def request_start(order, lengths):
    ends = jnp.cumsum(lengths)
    begins = ends - lengths
    return lax.optimization_barrier(jnp.max(jnp.where(begins[None, :] <= order[:, None], begins[None, :], 0), axis=1))

def reference(hidden_in, token_order, span_lengths, placement, norm_in, q_weight, k_weight, v_weight, q_gain, k_gain, o_weight, norm_mid, gate_weight, up_weight, down_weight):
    rows = hidden_in.shape[0]
    group = H // KVH
    xfull = hidden_in.astype(jnp.float32)
    normed = rms(xfull, norm_in).astype(jnp.bfloat16)
    begin = request_start(token_order, span_lengths)
    pos = token_order - begin
    query = jnp.dot(normed, q_weight, preferred_element_type=jnp.float32).reshape(rows, H, HD)
    keys = jnp.dot(normed, k_weight, preferred_element_type=jnp.float32).reshape(rows, KVH, HD)
    values = jnp.dot(normed, v_weight, preferred_element_type=jnp.float32).reshape(rows, KVH, HD).astype(jnp.bfloat16)
    qnorm = rotary(rms(query, q_gain), pos).astype(jnp.bfloat16)
    knorm = rotary(rms(keys, k_gain), pos).astype(jnp.bfloat16)
    kfloat = knorm.astype(jnp.float32)
    vfloat = values.astype(jnp.float32)
    block = 512 if rows % 512 == 0 else rows
    qblocks = qnorm.reshape(rows // block, block, KVH, group, HD)
    oblocks = token_order.reshape(rows // block, block)
    bblocks = begin.reshape(rows // block, block)
    scale = 1.0 / HD ** 0.5

    def attend(items):
        qpart, opart, bpart = items
        score = jnp.einsum('bkge,nke->bkgn', qpart.astype(jnp.float32), kfloat) * scale
        mask = (token_order[None, :] >= bpart[:, None]) & (token_order[None, :] <= opart[:, None])
        mask = mask[:, None, None, :]
        score = jnp.where(mask, score, -1e+30)
        top = lax.optimization_barrier(jnp.max(score, axis=-1, keepdims=True))
        weights = jnp.where(mask, jnp.exp(score - top), 0.0)
        total = lax.optimization_barrier(jnp.sum(weights, axis=-1))
        rounded = weights.astype(jnp.bfloat16).astype(jnp.float32)
        out = jnp.einsum('bkgn,nke->bkge', rounded, vfloat) / total[..., None]
        return out.astype(jnp.bfloat16)
    attn = lax.map(attend, (qblocks, oblocks, bblocks)).reshape(rows, H * HD)
    mid = (xfull + jnp.dot(attn, o_weight, preferred_element_type=jnp.float32)).astype(jnp.bfloat16)
    midf = mid.astype(jnp.float32)
    normed_mid = rms(midf, norm_mid).astype(jnp.bfloat16)
    gate = jnp.dot(normed_mid, gate_weight, preferred_element_type=jnp.float32)
    upper = jnp.dot(normed_mid, up_weight, preferred_element_type=jnp.float32)
    act = (jax.nn.silu(gate) * upper).astype(jnp.bfloat16)
    out = (midf + jnp.dot(act, down_weight, preferred_element_type=jnp.float32)).astype(jnp.bfloat16)
    hidden_out = jnp.zeros_like(out).at[token_order].set(out)
    stacked = jnp.stack([knorm, values], axis=2).reshape(rows, KVH * 2 * HD)
    slot_row = placement[token_order // BLK] * BLK + token_order % BLK
    kv_cache = jnp.zeros((NBLK * BLK, KVH * 2 * HD), jnp.bfloat16).at[slot_row].set(stacked)
    return (hidden_out, kv_cache.reshape(NBLK, BLK, KVH * 2 * HD))
```

```python
import jax
import jax.numpy as jnp
from jax import lax
from jax.sharding import PartitionSpec as P

HD = 128
BLK = 128


EPS = 1e-06
THETA = 1000000.0


def rms(values, gain):
    return values * lax.rsqrt(jnp.mean(values * values, axis=-1, keepdims=True) + EPS) * gain


def rotary(values, pos):
    half = values.shape[-1] // 2
    freq = THETA ** (-jnp.arange(half, dtype=jnp.float32) * 2.0 / values.shape[-1])
    angle = pos.astype(jnp.float32)[:, None] * freq[None, :]
    cosine = jnp.cos(angle)[:, None, :]
    sine = jnp.sin(angle)[:, None, :]
    first = values[..., :half]
    second = values[..., half:]
    return jnp.concatenate(
        [first * cosine - second * sine, second * cosine + first * sine], axis=-1
    )


def request_start(order, lengths):
    index = jnp.arange(lengths.shape[0])
    begins = jnp.sum(jnp.where(index[None, :] < index[:, None], lengths[None, :], 0), axis=1)
    return jnp.max(jnp.where(begins[None, :] <= order[:, None], begins[None, :], 0), axis=1)


def relay_cache(stacked, token_order, rows, seq_count):
    arrived, anchor = (
        lax.all_to_all(stacked, "seq", split_axis=0, concat_axis=0, tiled=True),
        lax.all_to_all(token_order, "seq", split_axis=0, concat_axis=0, tiled=True),
    )
    group_rows = rows // seq_count
    share = BLK // seq_count
    local_slot = jnp.arange(rows, dtype=jnp.int32) % group_rows // share
    target = local_slot * BLK + anchor % BLK
    cache = jnp.zeros(stacked.shape, jnp.bfloat16).at[target].set(arrived)
    return cache.reshape(rows // BLK, BLK, stacked.shape[1])


def body(
    hidden_in,
    token_order,
    span_lengths,
    placement,
    norm_in,
    q_weight,
    k_weight,
    v_weight,
    q_gain,
    k_gain,
    o_weight,
    norm_mid,
    gate_weight,
    up_weight,
    down_weight,
):
    rows, width = hidden_in.shape
    seq_count = lax.axis_size("seq")
    tp_count = lax.axis_size("tp")
    part = width // tp_count
    kv_heads = k_weight.shape[1] // HD
    q_heads = q_weight.shape[1] // HD
    group = q_heads // kv_heads
    xfull = hidden_in.astype(jnp.float32)
    normed = rms(xfull, norm_in).astype(jnp.bfloat16)
    begin = request_start(token_order, span_lengths)
    pos = token_order - begin
    query = jnp.dot(normed, q_weight, preferred_element_type=jnp.float32).reshape(rows, q_heads, HD)
    keys = jnp.dot(normed, k_weight, preferred_element_type=jnp.float32).reshape(rows, kv_heads, HD)
    values = (
        jnp.dot(normed, v_weight, preferred_element_type=jnp.float32)
        .reshape(rows, kv_heads, HD)
        .astype(jnp.bfloat16)
    )
    qnorm = rotary(rms(query, q_gain), pos).astype(jnp.bfloat16).reshape(rows, kv_heads, group, HD)
    knorm = rotary(rms(keys, k_gain), pos).astype(jnp.bfloat16)
    stacked = jnp.stack([knorm, values], axis=2).reshape(rows, kv_heads * 2 * HD)
    scale = 1.0 / HD**0.5
    start_best = jnp.full((rows, kv_heads, group), -1e30, jnp.float32)
    best = start_best
    piece_keys = lax.all_gather(knorm, "seq", axis=0, tiled=True)
    piece_values = lax.all_gather(values, "seq", axis=0, tiled=True)
    piece_order = lax.all_gather(token_order, "seq", axis=0, tiled=True)
    score = (
        jnp.einsum("qkge,nke->qkgn", qnorm, piece_keys, preferred_element_type=jnp.float32) * scale
    )
    mask = (piece_order[None, :] >= begin[:, None]) & (piece_order[None, :] <= token_order[:, None])
    mask = mask[:, None, None, :]
    score = jnp.where(mask, score, -1e30)
    new_best = jnp.maximum(best, jnp.max(score, axis=-1))
    weights = jnp.where(mask, jnp.exp(score - new_best[..., None]), 0.0)
    total = jnp.sum(weights, axis=-1)
    accum = jnp.einsum(
        "qkgn,nke->qkge",
        weights.astype(jnp.bfloat16),
        piece_values,
        preferred_element_type=jnp.float32,
    )
    best, total, accum = (new_best, total, accum)
    attn = (accum / total[..., None]).astype(jnp.bfloat16).reshape(rows, q_heads * HD)
    terms = jnp.dot(attn, o_weight, preferred_element_type=jnp.float32)
    column = lax.axis_index("tp") * part
    own_input = lax.dynamic_slice_in_dim(xfull, column, part, 1)
    mid = (
        own_input
        + lax.psum_scatter(
            terms.astype(jnp.bfloat16), "tp", scatter_dimension=1, tiled=True
        ).astype(jnp.float32)
    ).astype(jnp.bfloat16)
    mid_full = lax.all_gather(mid, "tp", axis=1, tiled=True)
    normed_mid = rms(mid_full.astype(jnp.float32), norm_mid).astype(jnp.bfloat16)
    gate = jnp.dot(normed_mid, gate_weight, preferred_element_type=jnp.float32)
    upper = jnp.dot(normed_mid, up_weight, preferred_element_type=jnp.float32)
    act = (jax.nn.silu(gate) * upper).astype(jnp.bfloat16)
    feed = lax.psum_scatter(
        jnp.dot(act, down_weight, preferred_element_type=jnp.float32).astype(jnp.bfloat16),
        "tp",
        scatter_dimension=1,
        tiled=True,
    ).astype(jnp.float32)
    out = (mid.astype(jnp.float32) + feed).astype(jnp.bfloat16)
    blocks_dev = rows // BLK
    share = BLK // seq_count
    slots = placement.reshape(seq_count, blocks_dev)
    send_rows = (
        slots[:, :, None] * share + jnp.arange(share, dtype=jnp.int32)[None, None, :]
    ).reshape(rows)
    arrived, anchor = (
        lax.all_to_all(out[send_rows], "seq", split_axis=0, concat_axis=0, tiled=True),
        lax.all_to_all(token_order[send_rows], "seq", split_axis=0, concat_axis=0, tiled=True),
    )
    local_row = anchor - lax.axis_index("seq") * rows
    hidden_out = jnp.zeros_like(out).at[local_row].set(arrived)
    kv_cache = relay_cache(stacked, token_order, rows, seq_count)
    return (hidden_out, kv_cache)


def solution(mesh):
    in_specs = (
        P("seq", None),
        P("seq"),
        P(),
        P(),
        P(),
        P(None, "tp"),
        P(None, "tp"),
        P(None, "tp"),
        P(),
        P(),
        P("tp", None),
        P(),
        P(None, "tp"),
        P(None, "tp"),
        P("tp", None),
    )
    out_specs = (P("seq", "tp"), P("seq", None, "tp"))
    return jax.shard_map(body, mesh=mesh, in_specs=in_specs, out_specs=out_specs, check_vma=False)
```

```python
import jax
import jax.numpy as jnp
from jax import lax
from jax.experimental import pallas as pl
from jax.experimental.pallas import tpu as pltpu
from jax.sharding import PartitionSpec as P

HD = 128
BLK = 128


EPS = 1e-06
THETA = 1000000.0


def rms(values, gain):
    return values * lax.rsqrt(jnp.mean(values * values, axis=-1, keepdims=True) + EPS) * gain


def rotary(values, pos):
    half = values.shape[-1] // 2
    freq = THETA ** (-jnp.arange(half, dtype=jnp.float32) * 2.0 / values.shape[-1])
    angle = pos.astype(jnp.float32)[:, None] * freq[None, :]
    cosine = jnp.cos(angle)[:, None, :]
    sine = jnp.sin(angle)[:, None, :]
    first = values[..., :half]
    second = values[..., half:]
    return jnp.concatenate(
        [first * cosine - second * sine, second * cosine + first * sine], axis=-1
    )


def request_start(order, lengths):
    index = jnp.arange(lengths.shape[0])
    begins = jnp.sum(jnp.where(index[None, :] < index[:, None], lengths[None, :], 0), axis=1)
    return jnp.max(jnp.where(begins[None, :] <= order[:, None], begins[None, :], 0), axis=1)


def relay_cache(stacked, token_order, rows, seq_count):
    arrived, anchor = (
        lax.all_to_all(stacked, "seq", split_axis=0, concat_axis=0, tiled=True),
        lax.all_to_all(token_order, "seq", split_axis=0, concat_axis=0, tiled=True),
    )
    group_rows = rows // seq_count
    share = BLK // seq_count
    local_slot = jnp.arange(rows, dtype=jnp.int32) % group_rows // share
    target = local_slot * BLK + anchor % BLK
    cache = jnp.zeros(stacked.shape, jnp.bfloat16).at[target].set(arrived)
    return cache.reshape(rows // BLK, BLK, stacked.shape[1])


def body(
    hidden_in,
    token_order,
    span_lengths,
    placement,
    norm_in,
    q_weight,
    k_weight,
    v_weight,
    q_gain,
    k_gain,
    o_weight,
    norm_mid,
    gate_weight,
    up_weight,
    down_weight,
):
    rows, width = hidden_in.shape
    seq_count = lax.axis_size("seq")
    tp_count = lax.axis_size("tp")
    part = width // tp_count
    kv_heads = k_weight.shape[1] // HD
    q_heads = q_weight.shape[1] // HD
    group = q_heads // kv_heads
    xfull = hidden_in.astype(jnp.float32)
    normed = rms(xfull, norm_in).astype(jnp.bfloat16)
    begin = request_start(token_order, span_lengths)
    pos = token_order - begin
    query = jnp.dot(normed, q_weight, preferred_element_type=jnp.float32).reshape(rows, q_heads, HD)
    keys = jnp.dot(normed, k_weight, preferred_element_type=jnp.float32).reshape(rows, kv_heads, HD)
    values = (
        jnp.dot(normed, v_weight, preferred_element_type=jnp.float32)
        .reshape(rows, kv_heads, HD)
        .astype(jnp.bfloat16)
    )
    qnorm = rotary(rms(query, q_gain), pos).astype(jnp.bfloat16).reshape(rows, kv_heads, group, HD)
    knorm = rotary(rms(keys, k_gain), pos).astype(jnp.bfloat16)
    stacked = jnp.stack([knorm, values], axis=2).reshape(rows, kv_heads * 2 * HD)
    scale = 1.0 / HD**0.5
    start_best = jnp.full((rows, kv_heads, group), -1e30, jnp.float32)
    best = start_best
    piece_keys = lax.all_gather(knorm, "seq", axis=0, tiled=True)
    piece_values = lax.all_gather(values, "seq", axis=0, tiled=True)
    piece_order = lax.all_gather(token_order, "seq", axis=0, tiled=True)
    score = (
        jnp.einsum("qkge,nke->qkgn", qnorm, piece_keys, preferred_element_type=jnp.float32) * scale
    )
    mask = (piece_order[None, :] >= begin[:, None]) & (piece_order[None, :] <= token_order[:, None])
    mask = mask[:, None, None, :]
    score = jnp.where(mask, score, -1e30)
    new_best = jnp.maximum(best, jnp.max(score, axis=-1))
    weights = jnp.where(mask, jnp.exp(score - new_best[..., None]), 0.0)
    total = jnp.sum(weights, axis=-1)
    accum = jnp.einsum(
        "qkgn,nke->qkge",
        weights.astype(jnp.bfloat16),
        piece_values,
        preferred_element_type=jnp.float32,
    )
    best, total, accum = (new_best, total, accum)
    attn = (accum / total[..., None]).astype(jnp.bfloat16).reshape(rows, q_heads * HD)
    terms = jnp.dot(attn, o_weight, preferred_element_type=jnp.float32)
    column = lax.axis_index("tp") * part
    own_input = lax.dynamic_slice_in_dim(xfull, column, part, 1)
    mid = (
        own_input
        + lax.psum_scatter(
            terms.astype(jnp.bfloat16), "tp", scatter_dimension=1, tiled=True
        ).astype(jnp.float32)
    ).astype(jnp.bfloat16)
    mid_full = lax.all_gather(mid, "tp", axis=1, tiled=True)
    normed_mid = rms(mid_full.astype(jnp.float32), norm_mid).astype(jnp.bfloat16)
    gate = jnp.dot(normed_mid, gate_weight, preferred_element_type=jnp.float32)
    upper = jnp.dot(normed_mid, up_weight, preferred_element_type=jnp.float32)
    act = (jax.nn.silu(gate) * upper).astype(jnp.bfloat16)
    feed = lax.psum_scatter(
        jnp.dot(act, down_weight, preferred_element_type=jnp.float32).astype(jnp.bfloat16),
        "tp",
        scatter_dimension=1,
        tiled=True,
    ).astype(jnp.float32)
    out = (mid.astype(jnp.float32) + feed).astype(jnp.bfloat16)
    blocks_dev = rows // BLK
    share = BLK // seq_count
    slots = placement.reshape(seq_count, blocks_dev)
    send_rows = (
        slots[:, :, None] * share + jnp.arange(share, dtype=jnp.int32)[None, None, :]
    ).reshape(rows)
    arrived, anchor = (
        lax.all_to_all(out[send_rows], "seq", split_axis=0, concat_axis=0, tiled=True),
        lax.all_to_all(token_order[send_rows], "seq", split_axis=0, concat_axis=0, tiled=True),
    )
    local_row = anchor - lax.axis_index("seq") * rows
    hidden_out = jnp.zeros_like(out).at[local_row].set(arrived)
    kv_cache = relay_cache(stacked, token_order, rows, seq_count)
    return (hidden_out, kv_cache)


BF = jnp.bfloat16
F32 = jnp.float32
VMEM_BYTES = 56 * 1024 * 1024


def project_kernel(x_ref, sel_ref, gain_ref, cos_ref, sin_ref, qg_ref, kg_ref, qw_ref, kw_ref, vw_ref,
                   xs_ref, q_ref, kv_ref, stacked_ref, normed):
    @pl.when(pl.program_id(0) == 0)
    def _():
        xs = jnp.dot(sel_ref[...], x_ref[...], preferred_element_type=F32)
        xs_ref[...] = xs.astype(BF)
        normed[...] = (
            xs * lax.rsqrt(jnp.mean(xs * xs, axis=-1, keepdims=True) + EPS) * gain_ref[...]
        ).astype(BF)

    cosine, sine = cos_ref[...], sin_ref[...]

    def turned(u, gain):
        u = u * lax.rsqrt(jnp.mean(u * u, axis=-1, keepdims=True) + EPS) * gain
        return (u * cosine + pltpu.roll(u, HD // 2, 1) * sine).astype(BF)

    base = normed[...]
    q = jnp.dot(base, qw_ref[...], preferred_element_type=F32)
    q_ref[0, :, :HD] = turned(q[:, :HD], qg_ref[...])
    q_ref[0, :, HD:] = turned(q[:, HD:], qg_ref[...])
    k = turned(jnp.dot(base, kw_ref[...], preferred_element_type=F32), kg_ref[...])
    v = jnp.dot(base, vw_ref[...], preferred_element_type=F32).astype(BF)
    kv = jnp.concatenate([k, v], axis=1)
    kv_ref[0] = kv
    stacked_ref[...] = lax.dot_general(
        sel_ref[...], kv, (((0,), (0,)), ((), ())), preferred_element_type=F32
    ).astype(BF)


def project(x, sel, gain, cosine, sine, qg, kg, qw, kw, vw):
    rows, width = x.shape
    heads = kw.shape[1] // HD
    whole = lambda shape: pl.BlockSpec(shape, lambda h: (0, 0))
    column = lambda cols: pl.BlockSpec((width, cols), lambda h: (0, h))
    head = pl.BlockSpec((1, rows, 2 * HD), lambda h: (h, 0, 0))
    return pl.pallas_call(
        project_kernel,
        grid=(heads,),
        in_specs=[whole((rows, width)), whole((rows, rows)), whole((1, width)), whole((rows, HD)),
                  whole((rows, HD)), whole((1, HD)), whole((1, HD)), column(2 * HD), column(HD), column(HD)],
        out_specs=[whole((rows, width)), head, head, pl.BlockSpec((rows, 2 * HD), lambda h: (0, h))],
        out_shape=[jax.ShapeDtypeStruct((rows, width), BF),
                   jax.ShapeDtypeStruct((heads, rows, 2 * HD), BF),
                   jax.ShapeDtypeStruct((heads, rows, 2 * HD), BF),
                   jax.ShapeDtypeStruct((rows, heads * 2 * HD), BF)],
        scratch_shapes=[pltpu.VMEM((rows, width), BF)],
        compiler_params=pltpu.CompilerParams(vmem_limit_bytes=VMEM_BYTES),
    )(x, sel, gain, cosine, sine, qg, kg, qw, kw, vw)


def greet(seq_count, sibling):
    barrier = pltpu.get_barrier_semaphore()
    me = lax.axis_index("seq")
    for k in range(1, seq_count):
        pl.semaphore_signal(barrier, inc=1, device_id={"seq": lax.rem(me + k, seq_count)})
    if sibling:
        pl.semaphore_signal(barrier, inc=1, device_id={"tp": 1 - lax.axis_index("tp")})
    pl.semaphore_wait(barrier, seq_count - 1 + (1 if sibling else 0))


def push(src, dst, send, recv, **where):
    return pltpu.make_async_remote_copy(
        src_ref=src, dst_ref=dst, send_sem=send, recv_sem=recv, device_id=where
    )


def exchange_kernel(n, kv_ref, q_ref, order_ref, cache_ref, kv_out, q_out, order_out, cache_out,
                    local, s1, r1, s2, r2, sq, rq, so, ro, sc, rc):
    me = lax.axis_index("seq")
    z, p = me // 4, lax.rem(me, 4)
    part = lambda seq: pl.ds(pl.multiple_of(seq * 16, 16), 16)
    own = [
        pltpu.make_async_copy(kv_ref.at[z], kv_out.at[:, part(me), :], local.at[0]),
        pltpu.make_async_copy(q_ref.at[z], q_out.at[:, part(z), :], local.at[1]),
        pltpu.make_async_copy(order_ref, order_out.at[me], local.at[2]),
        pltpu.make_async_copy(cache_ref.at[me], cache_out.at[me], local.at[3]),
    ]
    for copy in own:
        copy.start()
    greet(n, False)
    first, second, query, orders, caches = [], [], [], [], []
    for d in (1, 2, 3):
        there = lax.rem(z + d, 4)
        copy = push(kv_ref.at[there], kv_out.at[:, part(me), :], s1.at[d - 1], r1.at[d - 1], seq=there * 4 + p)
        copy.start()
        first.append(copy)
    for k in (1, 2, 3):
        copy = push(kv_ref.at[z], kv_out.at[:, part(me), :], s2.at[0, k - 1], r2.at[0, k - 1],
                    seq=z * 4 + lax.rem(p + k, 4))
        copy.start()
        second.append(copy)
    for k in range(1, n):
        copy = push(order_ref, order_out.at[me], so.at[k - 1], ro.at[k - 1], seq=lax.rem(me + k, n))
        copy.start()
        orders.append(copy)
    for d in (1, 2, 3):
        there = lax.rem(z + d, 4)
        copy = push(q_ref.at[there], q_out.at[:, part(z), :], sq.at[d - 1], rq.at[d - 1], seq=there * 4 + p)
        copy.start()
        query.append(copy)
    for d in (1, 3, 2):
        first[d - 1].wait_recv()
        rows = part(lax.rem(z + 4 - d, 4) * 4 + p)
        for k in (1, 2, 3):
            copy = push(kv_out.at[:, rows, :], kv_out.at[:, rows, :], s2.at[d, k - 1], r2.at[d, k - 1],
                        seq=z * 4 + lax.rem(p + k, 4))
            copy.start()
            second.append(copy)
    for k in range(1, n):
        there = lax.rem(me + k, n)
        copy = push(cache_ref.at[there], cache_out.at[me], sc.at[k - 1], rc.at[k - 1], seq=there)
        copy.start()
        caches.append(copy)
    for copy in own:
        copy.wait()
    for copy in first:
        copy.wait_send()
    for copy in second + query + orders + caches:
        copy.wait()


def exchange(kv, q, orders, cache, n):
    heads = kv.shape[0]
    dma = pltpu.SemaphoreType.DMA
    anywhere = pl.BlockSpec(memory_space=pl.ANY)
    width = kv.shape[-1]
    return pl.pallas_call(
        lambda *refs: exchange_kernel(n, *refs),
        in_specs=[anywhere] * 4,
        out_specs=[anywhere] * 4,
        out_shape=[jax.ShapeDtypeStruct((n, n * 16, width), BF),
                   jax.ShapeDtypeStruct((n, 4 * 16, width), BF),
                   jax.ShapeDtypeStruct((n,) + orders.shape, jnp.int32),
                   jax.ShapeDtypeStruct(cache.shape, BF)],
        scratch_shapes=[dma((4,)), dma((3,)), dma((3,)), dma((4, 3)), dma((4, 3)), dma((3,)), dma((3,)),
                        dma((n - 1,)), dma((n - 1,)), dma((n - 1,)), dma((n - 1,))],
        compiler_params=pltpu.CompilerParams(collective_id=0, has_side_effects=True),
    )(kv, q, orders, cache)


def attend_kernel(low_ref, q_ref, kv_ref, info_ref, key_ref, out_ref):
    i = pl.program_id(0)
    q = q_ref[...].reshape(128, 2 * HD)
    both = jnp.concatenate([q[:, :HD], q[:, HD:]], axis=0)
    token, begin = info_ref[:, 0:1], info_ref[:, 1:2]
    scale = 1.0 / HD**0.5

    key_all = key_ref[...]
    which = lax.broadcasted_iota(jnp.int32, key_all.shape, 0)

    def step(j, carry):
        best, total, accum = carry
        kv = kv_ref[pl.ds(2 * j, 2)].reshape(512, 2 * HD)
        score = lax.dot_general(
            both, kv[:, :HD], (((1,), (1,)), ((), ())), preferred_element_type=F32
        ) * scale
        keys = jnp.sum(jnp.where(which == j, key_all, 0), axis=0, keepdims=True)
        mask = (keys >= begin) & (keys <= token)
        score = jnp.where(jnp.concatenate([mask, mask], axis=0), score, -1e30)
        new_best = jnp.maximum(best, jnp.max(score, axis=1, keepdims=True))
        weights = jnp.exp(score - new_best)
        shrink = jnp.exp(best - new_best)
        total = total * shrink + jnp.sum(weights, axis=1, keepdims=True)
        accum = accum * shrink + jnp.dot(weights.astype(BF), kv[:, HD:], preferred_element_type=F32)
        return new_best, total, accum

    start = (jnp.full((256, 1), -1e30, F32), jnp.zeros((256, 1), F32), jnp.zeros((256, HD), F32))
    _, total, accum = lax.fori_loop(low_ref[i], i + 1, step, start)
    attn = (accum / total).astype(BF)
    out_ref[...] = jnp.concatenate([attn[:128], attn[128:]], axis=1).reshape(2, 64, 2 * HD)


def attend(low, q, kv, info, keys):
    tiles = q.shape[0] // 2
    block = pl.BlockSpec((2, 64, 2 * HD), lambda i, low: (i, 0, 0))
    return pl.pallas_call(
        attend_kernel,
        grid_spec=pltpu.PrefetchScalarGridSpec(
            num_scalar_prefetch=1,
            grid=(tiles,),
            in_specs=[block, pl.BlockSpec(kv.shape, lambda i, low: (0, 0, 0)),
                      pl.BlockSpec((128, 2), lambda i, low: (i, 0)),
                      pl.BlockSpec(keys.shape, lambda i, low: (0, 0))],
            out_specs=block,
        ),
        out_shape=jax.ShapeDtypeStruct(q.shape, BF),
        compiler_params=pltpu.CompilerParams(vmem_limit_bytes=VMEM_BYTES),
    )(low, q, kv, info, keys)


def finish_kernel(n, attn_ref, xs_ref, gain_ref, place_ref, wo_hbm, wg_hbm, wu_hbm, wd_hbm, out_ref,
                  wo, wg, wu, wd, attn, terms, sent, came, mid, normed, act, half_out, half_in, ready, arrived,
                  wsem, local, sa, ra, st, rt, sf, rf, sx, rx):
    me, t = lax.axis_index("seq"), lax.axis_index("tp")
    z, p = me // 4, lax.rem(me, 4)
    part = lambda seq: pl.ds(pl.multiple_of(seq * 16, 16), 16)
    loads = [pltpu.make_async_copy(a, b, wsem.at[i])
             for i, (a, b) in enumerate(((wo_hbm, wo), (wg_hbm, wg), (wu_hbm, wu), (wd_hbm, wd)))]
    for load in loads:
        load.start()
    keep = pltpu.make_async_copy(attn_ref.at[:, part(z), :], attn.at[z], local.at[0])
    keep.start()
    greet(n, True)
    moves = []
    for d in (1, 2, 3):
        there = lax.rem(z + d, 4)
        copy = push(attn_ref.at[:, part(there), :], attn.at[z], sa.at[d - 1], ra.at[d - 1], seq=there * 4 + p)
        copy.start()
        moves.append(copy)
    loads[0].wait()
    keep.wait()
    for copy in moves:
        copy.wait()
    rows, width = xs_ref.shape
    part_width = width // 2
    tile = 256
    column = lambda j: pl.ds(pl.multiple_of(j * tile, tile), tile)

    @pl.loop(0, width // tile)
    def _(j):
        result = jnp.zeros((rows, tile), F32)
        for h in range(4):
            result += jnp.dot(attn[h].reshape(rows, 2 * HD), wo[h * 256:(h + 1) * 256, column(j)],
                              preferred_element_type=F32)
        sent[:, column(j)] = result.astype(BF)

    swap = push(sent, came, st.at[0], rt.at[0], tp=1 - t)
    swap.start()
    swap.wait()
    full = xs_ref[...].astype(F32) + (sent[...].astype(F32) + came[...].astype(F32))
    mid[...] = full.astype(BF)
    full = mid[...].astype(F32)
    normed[...] = (
        full * lax.rsqrt(jnp.mean(full * full, axis=-1, keepdims=True) + EPS) * gain_ref[...]
    ).astype(BF)
    loads[1].wait()
    loads[2].wait()

    @pl.loop(0, act.shape[1] // tile)
    def _(j):
        gate = jnp.dot(normed[...], wg[:, column(j)], preferred_element_type=F32)
        upper = jnp.dot(normed[...], wu[:, column(j)], preferred_element_type=F32)
        act[:, column(j)] = (gate * jax.nn.sigmoid(gate) * upper).astype(BF)

    loads[3].wait()
    steps = part_width // tile

    @pl.loop(0, steps)
    def _(j):
        half_out[:, column(j)] = jnp.dot(
            act[...], wd[:, column((1 - t) * steps + j)], preferred_element_type=F32
        ).astype(BF)

    swap = push(half_out, half_in, sf.at[0], rf.at[0], tp=1 - t)
    swap.start()

    @pl.loop(0, steps)
    def _(j):
        terms[:, column(j)] = jnp.dot(act[...], wd[:, column(t * steps + j)], preferred_element_type=F32)

    swap.wait()

    @pl.loop(0, steps)
    def _(j):
        out = mid[:, column(t * steps + j)].astype(F32) + (
            terms[:, column(j)] + half_in[:, column(j)].astype(F32)
        )
        ready[:, :, column(j)] = out.astype(BF).reshape(n, rows // n, tile)

    keep = pltpu.make_async_copy(ready.at[me], arrived.at[me], local.at[1])
    keep.start()
    moves = []
    for k in range(1, n):
        there = lax.rem(me + k, n)
        copy = push(ready.at[there], arrived.at[me], sx.at[k - 1], rx.at[k - 1], seq=there)
        copy.start()
        moves.append(copy)
    keep.wait()
    for copy in moves:
        copy.wait()

    @pl.loop(0, steps)
    def _(j):
        out_ref[:, column(j)] = jnp.dot(
            place_ref[...], arrived[:, :, column(j)].reshape(rows, tile), preferred_element_type=F32
        ).astype(BF)


def finish(attn, xs, gain, place, wo, wg, wu, wd, n):
    rows, width = xs.shape
    half, hidden = width // 2, wg.shape[1]
    dma = pltpu.SemaphoreType.DMA
    vmem = pl.BlockSpec(memory_space=pltpu.VMEM)
    anywhere = pl.BlockSpec(memory_space=pl.ANY)
    room = lambda *shape: pltpu.VMEM(shape, BF)
    return pl.pallas_call(
        lambda *refs: finish_kernel(n, *refs),
        in_specs=[anywhere, vmem, vmem, vmem] + [anywhere] * 4,
        out_specs=vmem,
        out_shape=jax.ShapeDtypeStruct((rows, half), BF),
        scratch_shapes=[room(*wo.shape), room(*wg.shape), room(*wu.shape), room(*wd.shape),
                        room(4, n, rows // n, 2 * HD), pltpu.VMEM((rows, half), F32),
                        room(rows, width), room(rows, width), room(rows, width), room(rows, width),
                        room(rows, hidden), room(rows, half), room(rows, half),
                        room(n, rows // n, half), room(n, rows // n, half),
                        dma((4,)), dma((2,)), dma((3,)), dma((3,)), dma((1,)), dma((1,)), dma((1,)), dma((1,)),
                        dma((n - 1,)), dma((n - 1,))],
        compiler_params=pltpu.CompilerParams(
            collective_id=1, has_side_effects=True, vmem_limit_bytes=VMEM_BYTES
        ),
    )(attn, xs, gain, place, wo, wg, wu, wd)


def fast_body(
    hidden_in, token_order, span_lengths, placement, norm_in, q_weight, k_weight, v_weight, q_gain, k_gain,
    o_weight, norm_mid, gate_weight, up_weight, down_weight,
):
    rows, width = hidden_in.shape
    n = lax.axis_size("seq")
    me = lax.axis_index("seq")
    share = BLK // n
    slot_rows = (placement[:, None] * share + jnp.arange(share, dtype=jnp.int32)[None, :]).reshape(rows)
    chosen = slot_rows[:, None] == jnp.arange(rows, dtype=jnp.int32)[None, :]
    order = jnp.sum(jnp.where(chosen, token_order[None, :], 0), axis=1)
    pos = order - request_start(order, span_lengths)
    half = HD // 2
    freq = THETA ** (-jnp.arange(half, dtype=F32) * 2.0 / HD)
    angle = pos.astype(F32)[:, None] * freq[None, :]
    cosine, sine = jnp.cos(angle), jnp.sin(angle)
    cosine = jnp.concatenate([cosine, cosine], axis=1)
    sine = jnp.concatenate([-sine, sine], axis=1)
    xs, q, kv, stacked = project(
        hidden_in, chosen.astype(BF), norm_in[None, :], cosine, sine, q_gain[None, :], k_gain[None, :],
        q_weight, k_weight, v_weight,
    )
    group = rows // n
    split = lambda a: a.reshape(a.shape[0], n, group, a.shape[2])
    orders = jnp.concatenate(
        [order[None, :], token_order[None, :], jnp.zeros((6, rows), jnp.int32)], axis=0
    )
    kv_all, q_all, orders_all, cache_all = exchange(
        split(kv), split(q), orders, stacked.reshape(n, group, stacked.shape[1]), n
    )
    by_pair = orders_all[:, 0, :].reshape(n, n, group)
    keys = by_pair.transpose(1, 0, 2).reshape(n // 2, 2 * n * group)
    mine = lax.dynamic_index_in_dim(by_pair.reshape(4, 4, n, group), lax.rem(me, 4), 1, keepdims=False)
    token = mine.transpose(1, 0, 2).reshape(n * 4 * group)
    info = jnp.stack([token, request_start(token, span_lengths)], axis=1)
    low = request_start(jnp.arange(n // 2, dtype=jnp.int32) * (2 * rows), span_lengths) // (2 * rows)
    attn = attend(low, q_all, kv_all, info, keys)
    row_ids = jnp.arange(rows, dtype=jnp.int32)
    landed = lax.dynamic_index_in_dim(by_pair, me, 1, keepdims=False).reshape(rows) - me * rows
    place = (row_ids[:, None] == landed[None, :]).astype(BF)
    hidden_out = finish(
        attn, xs, norm_mid[None, :], place, o_weight, gate_weight, up_weight, down_weight, n
    )
    anchor = lax.dynamic_index_in_dim(
        orders_all[:, 1, :].reshape(n, n, group), me, 1, keepdims=False
    ).reshape(rows)
    target = row_ids % group // share * BLK + anchor % BLK
    to_cache = (row_ids[:, None] == target[None, :]).astype(BF)
    kv_cache = jnp.dot(
        to_cache, cache_all.reshape(rows, stacked.shape[1]), preferred_element_type=F32
    ).astype(BF).reshape(rows // BLK, BLK, stacked.shape[1])
    return (hidden_out, kv_cache)


def solution(mesh):
    in_specs = (
        P("seq", None),
        P("seq"),
        P(),
        P(),
        P(),
        P(None, "tp"),
        P(None, "tp"),
        P(None, "tp"),
        P(),
        P(),
        P("tp", None),
        P(),
        P(None, "tp"),
        P(None, "tp"),
        P("tp", None),
    )
    out_specs = (P("seq", "tp"), P("seq", None, "tp"))
    chosen = fast_body if mesh.shape["seq"] == 16 and mesh.shape["tp"] == 2 else body
    return jax.shard_map(chosen, mesh=mesh, in_specs=in_specs, out_specs=out_specs, check_vma=False)
```

```python
import jax
import jax.numpy as jnp
from jax import lax
from jax.experimental import pallas as pl
from jax.experimental.pallas import tpu as pltpu
from jax.sharding import PartitionSpec as P

HD = 128
BLK = 128


EPS = 1e-06
THETA = 1000000.0


def rms(values, gain):
    return values * lax.rsqrt(jnp.mean(values * values, axis=-1, keepdims=True) + EPS) * gain


def rotary(values, pos):
    half = values.shape[-1] // 2
    freq = THETA ** (-jnp.arange(half, dtype=jnp.float32) * 2.0 / values.shape[-1])
    angle = pos.astype(jnp.float32)[:, None] * freq[None, :]
    cosine = jnp.cos(angle)[:, None, :]
    sine = jnp.sin(angle)[:, None, :]
    first = values[..., :half]
    second = values[..., half:]
    return jnp.concatenate(
        [first * cosine - second * sine, second * cosine + first * sine], axis=-1
    )


def request_start(order, lengths):
    index = jnp.arange(lengths.shape[0])
    begins = jnp.sum(jnp.where(index[None, :] < index[:, None], lengths[None, :], 0), axis=1)
    return jnp.max(jnp.where(begins[None, :] <= order[:, None], begins[None, :], 0), axis=1)


def relay_cache(stacked, token_order, rows, seq_count):
    arrived, anchor = (
        lax.all_to_all(stacked, "seq", split_axis=0, concat_axis=0, tiled=True),
        lax.all_to_all(token_order, "seq", split_axis=0, concat_axis=0, tiled=True),
    )
    group_rows = rows // seq_count
    share = BLK // seq_count
    local_slot = jnp.arange(rows, dtype=jnp.int32) % group_rows // share
    target = local_slot * BLK + anchor % BLK
    cache = jnp.zeros(stacked.shape, jnp.bfloat16).at[target].set(arrived)
    return cache.reshape(rows // BLK, BLK, stacked.shape[1])


def body(
    hidden_in,
    token_order,
    span_lengths,
    placement,
    norm_in,
    q_weight,
    k_weight,
    v_weight,
    q_gain,
    k_gain,
    o_weight,
    norm_mid,
    gate_weight,
    up_weight,
    down_weight,
):
    rows, width = hidden_in.shape
    seq_count = lax.axis_size("seq")
    tp_count = lax.axis_size("tp")
    part = width // tp_count
    kv_heads = k_weight.shape[1] // HD
    q_heads = q_weight.shape[1] // HD
    group = q_heads // kv_heads
    xfull = hidden_in.astype(jnp.float32)
    normed = rms(xfull, norm_in).astype(jnp.bfloat16)
    begin = request_start(token_order, span_lengths)
    pos = token_order - begin
    query = jnp.dot(normed, q_weight, preferred_element_type=jnp.float32).reshape(rows, q_heads, HD)
    keys = jnp.dot(normed, k_weight, preferred_element_type=jnp.float32).reshape(rows, kv_heads, HD)
    values = (
        jnp.dot(normed, v_weight, preferred_element_type=jnp.float32)
        .reshape(rows, kv_heads, HD)
        .astype(jnp.bfloat16)
    )
    qnorm = rotary(rms(query, q_gain), pos).astype(jnp.bfloat16).reshape(rows, kv_heads, group, HD)
    knorm = rotary(rms(keys, k_gain), pos).astype(jnp.bfloat16)
    stacked = jnp.stack([knorm, values], axis=2).reshape(rows, kv_heads * 2 * HD)
    scale = 1.0 / HD**0.5
    start_best = jnp.full((rows, kv_heads, group), -1e30, jnp.float32)
    best = start_best
    piece_keys = lax.all_gather(knorm, "seq", axis=0, tiled=True)
    piece_values = lax.all_gather(values, "seq", axis=0, tiled=True)
    piece_order = lax.all_gather(token_order, "seq", axis=0, tiled=True)
    score = (
        jnp.einsum("qkge,nke->qkgn", qnorm, piece_keys, preferred_element_type=jnp.float32) * scale
    )
    mask = (piece_order[None, :] >= begin[:, None]) & (piece_order[None, :] <= token_order[:, None])
    mask = mask[:, None, None, :]
    score = jnp.where(mask, score, -1e30)
    new_best = jnp.maximum(best, jnp.max(score, axis=-1))
    weights = jnp.where(mask, jnp.exp(score - new_best[..., None]), 0.0)
    total = jnp.sum(weights, axis=-1)
    accum = jnp.einsum(
        "qkgn,nke->qkge",
        weights.astype(jnp.bfloat16),
        piece_values,
        preferred_element_type=jnp.float32,
    )
    best, total, accum = (new_best, total, accum)
    attn = (accum / total[..., None]).astype(jnp.bfloat16).reshape(rows, q_heads * HD)
    terms = jnp.dot(attn, o_weight, preferred_element_type=jnp.float32)
    column = lax.axis_index("tp") * part
    own_input = lax.dynamic_slice_in_dim(xfull, column, part, 1)
    mid = (
        own_input
        + lax.psum_scatter(
            terms.astype(jnp.bfloat16), "tp", scatter_dimension=1, tiled=True
        ).astype(jnp.float32)
    ).astype(jnp.bfloat16)
    mid_full = lax.all_gather(mid, "tp", axis=1, tiled=True)
    normed_mid = rms(mid_full.astype(jnp.float32), norm_mid).astype(jnp.bfloat16)
    gate = jnp.dot(normed_mid, gate_weight, preferred_element_type=jnp.float32)
    upper = jnp.dot(normed_mid, up_weight, preferred_element_type=jnp.float32)
    act = (jax.nn.silu(gate) * upper).astype(jnp.bfloat16)
    feed = lax.psum_scatter(
        jnp.dot(act, down_weight, preferred_element_type=jnp.float32).astype(jnp.bfloat16),
        "tp",
        scatter_dimension=1,
        tiled=True,
    ).astype(jnp.float32)
    out = (mid.astype(jnp.float32) + feed).astype(jnp.bfloat16)
    blocks_dev = rows // BLK
    share = BLK // seq_count
    slots = placement.reshape(seq_count, blocks_dev)
    send_rows = (
        slots[:, :, None] * share + jnp.arange(share, dtype=jnp.int32)[None, None, :]
    ).reshape(rows)
    arrived, anchor = (
        lax.all_to_all(out[send_rows], "seq", split_axis=0, concat_axis=0, tiled=True),
        lax.all_to_all(token_order[send_rows], "seq", split_axis=0, concat_axis=0, tiled=True),
    )
    local_row = anchor - lax.axis_index("seq") * rows
    hidden_out = jnp.zeros_like(out).at[local_row].set(arrived)
    kv_cache = relay_cache(stacked, token_order, rows, seq_count)
    return (hidden_out, kv_cache)


BF = jnp.bfloat16
F32 = jnp.float32
VMEM_BYTES = 56 * 1024 * 1024


def project_kernel(x_ref, sel_ref, gain_ref, cos_ref, sin_ref, qg_ref, kg_ref, qw_ref, kw_ref, vw_ref,
                   xs_ref, q_ref, kv_ref, stacked_ref, normed):
    @pl.when(pl.program_id(0) == 0)
    def _():
        xs = jnp.dot(sel_ref[...], x_ref[...], preferred_element_type=F32)
        xs_ref[...] = xs.astype(BF)
        normed[...] = (
            xs * lax.rsqrt(jnp.mean(xs * xs, axis=-1, keepdims=True) + EPS) * gain_ref[...]
        ).astype(BF)

    cosine, sine = cos_ref[...], sin_ref[...]

    def turned(u, gain):
        u = u * lax.rsqrt(jnp.mean(u * u, axis=-1, keepdims=True) + EPS) * gain
        return (u * cosine + pltpu.roll(u, HD // 2, 1) * sine).astype(BF)

    base = normed[...]
    q = jnp.dot(base, qw_ref[...], preferred_element_type=F32)
    q_ref[0, :, :HD] = turned(q[:, :HD], qg_ref[...])
    q_ref[0, :, HD:] = turned(q[:, HD:], qg_ref[...])
    k = turned(jnp.dot(base, kw_ref[...], preferred_element_type=F32), kg_ref[...])
    v = jnp.dot(base, vw_ref[...], preferred_element_type=F32).astype(BF)
    kv = jnp.concatenate([k, v], axis=1)
    kv_ref[0] = kv
    stacked_ref[...] = lax.dot_general(
        sel_ref[...], kv, (((0,), (0,)), ((), ())), preferred_element_type=F32
    ).astype(BF)


def project(x, sel, gain, cosine, sine, qg, kg, qw, kw, vw):
    rows, width = x.shape
    heads = kw.shape[1] // HD
    whole = lambda shape: pl.BlockSpec(shape, lambda h: (0, 0))
    column = lambda cols: pl.BlockSpec((width, cols), lambda h: (0, h))
    head = pl.BlockSpec((1, rows, 2 * HD), lambda h: (h, 0, 0))
    return pl.pallas_call(
        project_kernel,
        grid=(heads,),
        in_specs=[whole((rows, width)), whole((rows, rows)), whole((1, width)), whole((rows, HD)),
                  whole((rows, HD)), whole((1, HD)), whole((1, HD)), column(2 * HD), column(HD), column(HD)],
        out_specs=[whole((rows, width)), head, head, pl.BlockSpec((rows, 2 * HD), lambda h: (0, h))],
        out_shape=[jax.ShapeDtypeStruct((rows, width), BF),
                   jax.ShapeDtypeStruct((heads, rows, 2 * HD), BF),
                   jax.ShapeDtypeStruct((heads, rows, 2 * HD), BF),
                   jax.ShapeDtypeStruct((rows, heads * 2 * HD), BF)],
        scratch_shapes=[pltpu.VMEM((rows, width), BF)],
        compiler_params=pltpu.CompilerParams(vmem_limit_bytes=VMEM_BYTES),
    )(x, sel, gain, cosine, sine, qg, kg, qw, kw, vw)


def greet(seq_count, sibling):
    barrier = pltpu.get_barrier_semaphore()
    me = lax.axis_index("seq")
    for k in range(1, seq_count):
        pl.semaphore_signal(barrier, inc=1, device_id={"seq": lax.rem(me + k, seq_count)})
    if sibling:
        pl.semaphore_signal(barrier, inc=1, device_id={"tp": 1 - lax.axis_index("tp")})
    pl.semaphore_wait(barrier, seq_count - 1 + (1 if sibling else 0))


def push(src, dst, send, recv, **where):
    return pltpu.make_async_remote_copy(
        src_ref=src, dst_ref=dst, send_sem=send, recv_sem=recv, device_id=where
    )


def exchange_kernel(n, kv_ref, q_ref, order_ref, kv_out, q_out, order_out,
                    local, s1, r1, s2, r2, sq, rq, so, ro):
    me = lax.axis_index("seq")
    z, p = me // 4, lax.rem(me, 4)
    part = lambda seq: pl.ds(pl.multiple_of(seq * 16, 16), 16)
    own = [
        pltpu.make_async_copy(kv_ref.at[z], kv_out.at[:, part(me), :], local.at[0]),
        pltpu.make_async_copy(q_ref.at[z], q_out.at[:, part(z), :], local.at[1]),
        pltpu.make_async_copy(order_ref, order_out.at[me], local.at[2]),
    ]
    for copy in own:
        copy.start()
    greet(n, False)
    first, second, query, orders = [], [], [], []
    for d in (1, 2, 3):
        there = lax.rem(z + d, 4)
        copy = push(kv_ref.at[there], kv_out.at[:, part(me), :], s1.at[d - 1], r1.at[d - 1], seq=there * 4 + p)
        copy.start()
        first.append(copy)
    for k in (1, 2, 3):
        copy = push(kv_ref.at[z], kv_out.at[:, part(me), :], s2.at[0, k - 1], r2.at[0, k - 1],
                    seq=z * 4 + lax.rem(p + k, 4))
        copy.start()
        second.append(copy)
    for k in range(1, n):
        copy = push(order_ref, order_out.at[me], so.at[k - 1], ro.at[k - 1], seq=lax.rem(me + k, n))
        copy.start()
        orders.append(copy)
    for d in (1, 2, 3):
        there = lax.rem(z + d, 4)
        copy = push(q_ref.at[there], q_out.at[:, part(z), :], sq.at[d - 1], rq.at[d - 1], seq=there * 4 + p)
        copy.start()
        query.append(copy)
    for d in (1, 3, 2):
        first[d - 1].wait_recv()
        rows = part(lax.rem(z + 4 - d, 4) * 4 + p)
        for k in (1, 2, 3):
            copy = push(kv_out.at[:, rows, :], kv_out.at[:, rows, :], s2.at[d, k - 1], r2.at[d, k - 1],
                        seq=z * 4 + lax.rem(p + k, 4))
            copy.start()
            second.append(copy)
    for copy in own:
        copy.wait()
    for copy in first:
        copy.wait_send()
    for copy in second + query + orders:
        copy.wait()


def exchange(kv, q, orders, n):
    heads = kv.shape[0]
    dma = pltpu.SemaphoreType.DMA
    anywhere = pl.BlockSpec(memory_space=pl.ANY)
    width = kv.shape[-1]
    return pl.pallas_call(
        lambda *refs: exchange_kernel(n, *refs),
        in_specs=[anywhere] * 3,
        out_specs=[anywhere] * 3,
        out_shape=[jax.ShapeDtypeStruct((n, n * 16, width), BF),
                   jax.ShapeDtypeStruct((n, 4 * 16, width), BF),
                   jax.ShapeDtypeStruct((n,) + orders.shape, jnp.int32)],
        scratch_shapes=[dma((3,)), dma((3,)), dma((3,)), dma((4, 3)), dma((4, 3)), dma((3,)), dma((3,)),
                        dma((n - 1,)), dma((n - 1,))],
        compiler_params=pltpu.CompilerParams(collective_id=0, has_side_effects=True),
    )(kv, q, orders)


def attend_kernel(low_ref, q_ref, kv_ref, info_ref, key_ref, out_ref):
    i = pl.program_id(0)
    q = q_ref[...].reshape(128, 2 * HD)
    both = jnp.concatenate([q[:, :HD], q[:, HD:]], axis=0)
    token, begin = info_ref[:, 0:1], info_ref[:, 1:2]
    scale = 1.0 / HD**0.5

    key_all = key_ref[...]
    which = lax.broadcasted_iota(jnp.int32, key_all.shape, 0)

    def step(j, carry):
        best, total, accum = carry
        kv = kv_ref[pl.ds(2 * j, 2)].reshape(512, 2 * HD)
        score = lax.dot_general(
            both, kv[:, :HD], (((1,), (1,)), ((), ())), preferred_element_type=F32
        ) * scale
        keys = jnp.sum(jnp.where(which == j, key_all, 0), axis=0, keepdims=True)
        mask = (keys >= begin) & (keys <= token)
        score = jnp.where(jnp.concatenate([mask, mask], axis=0), score, -1e30)
        new_best = jnp.maximum(best, jnp.max(score, axis=1, keepdims=True))
        weights = jnp.exp(score - new_best)
        shrink = jnp.exp(best - new_best)
        total = total * shrink + jnp.sum(weights, axis=1, keepdims=True)
        accum = accum * shrink + jnp.dot(weights.astype(BF), kv[:, HD:], preferred_element_type=F32)
        return new_best, total, accum

    start = (jnp.full((256, 1), -1e30, F32), jnp.zeros((256, 1), F32), jnp.zeros((256, HD), F32))
    _, total, accum = lax.fori_loop(low_ref[i], i + 1, step, start)
    attn = (accum / total).astype(BF)
    out_ref[...] = jnp.concatenate([attn[:128], attn[128:]], axis=1).reshape(2, 64, 2 * HD)


def attend(low, q, kv, info, keys):
    tiles = q.shape[0] // 2
    block = pl.BlockSpec((2, 64, 2 * HD), lambda i, low: (i, 0, 0))
    return pl.pallas_call(
        attend_kernel,
        grid_spec=pltpu.PrefetchScalarGridSpec(
            num_scalar_prefetch=1,
            grid=(tiles,),
            in_specs=[block, pl.BlockSpec(kv.shape, lambda i, low: (0, 0, 0)),
                      pl.BlockSpec((128, 2), lambda i, low: (i, 0)),
                      pl.BlockSpec(keys.shape, lambda i, low: (0, 0))],
            out_specs=block,
        ),
        out_shape=jax.ShapeDtypeStruct(q.shape, BF),
        compiler_params=pltpu.CompilerParams(vmem_limit_bytes=VMEM_BYTES),
    )(low, q, kv, info, keys)


def finish_kernel(n, attn_ref, xs_ref, gain_ref, cache_ref, wo_hbm, wg_hbm, wu_hbm, wd_hbm, arrived, cache_out,
                  wo, wg, wu, wd, attn, sent, came, mid, normed, act, half_out, half_in, ready,
                  wsem, local, sa, ra, st, rt, sf, rf, sx, rx, sc, rc):
    me, t = lax.axis_index("seq"), lax.axis_index("tp")
    z, p = me // 4, lax.rem(me, 4)
    part = lambda seq: pl.ds(pl.multiple_of(seq * 16, 16), 16)
    loads = [pltpu.make_async_copy(a, b, wsem.at[i])
             for i, (a, b) in enumerate(((wo_hbm, wo), (wg_hbm, wg), (wu_hbm, wu), (wd_hbm, wd)))]
    for load in loads:
        load.start()
    keep = pltpu.make_async_copy(attn_ref.at[:, part(z), :], attn.at[z], local.at[0])
    keep.start()
    late = [pltpu.make_async_copy(cache_ref.at[me], cache_out.at[me], local.at[1])]
    late[0].start()
    greet(n, True)
    moves = []
    for d in (1, 2, 3):
        there = lax.rem(z + d, 4)
        copy = push(attn_ref.at[:, part(there), :], attn.at[z], sa.at[d - 1], ra.at[d - 1], seq=there * 4 + p)
        copy.start()
        moves.append(copy)
    for k in range(1, n):
        there = lax.rem(me + k, n)
        copy = push(cache_ref.at[there], cache_out.at[me], sc.at[k - 1], rc.at[k - 1], seq=there)
        copy.start()
        late.append(copy)
    loads[0].wait()
    keep.wait()
    for copy in moves:
        copy.wait()
    rows, width = xs_ref.shape
    tile = 256
    column = lambda j: pl.ds(pl.multiple_of(j * tile, tile), tile)
    swaps = []
    for j in range(width // tile):
        result = jnp.zeros((rows, tile), F32)
        for h in range(4):
            result += jnp.dot(attn[h].reshape(rows, 2 * HD), wo[h * 256:(h + 1) * 256, j * tile:(j + 1) * tile],
                              preferred_element_type=F32)
        sent[:, j * tile:(j + 1) * tile] = result.astype(BF)
        if j % 2:
            c = j // 2
            both = pl.ds(c * 2 * tile, 2 * tile)
            swap = push(sent.at[:, both], came.at[:, both], st.at[c], rt.at[c], tp=1 - t)
            swap.start()
            swaps.append(swap)
    square = jnp.zeros((rows, 1), F32)
    for c, swap in enumerate(swaps):
        swap.wait()
        cols = slice(c * 2 * tile, (c + 1) * 2 * tile)
        piece = xs_ref[:, cols].astype(F32) + (sent[:, cols].astype(F32) + came[:, cols].astype(F32))
        piece = piece.astype(BF)
        mid[:, cols] = piece
        piece = piece.astype(F32)
        square += jnp.sum(piece * piece, axis=-1, keepdims=True)
    factor = lax.rsqrt(square / width + EPS)
    for c in range(len(swaps)):
        cols = slice(c * 2 * tile, (c + 1) * 2 * tile)
        normed[:, cols] = (mid[:, cols].astype(F32) * factor * gain_ref[:, cols]).astype(BF)
    loads[1].wait()
    loads[2].wait()

    @pl.loop(0, act.shape[1] // tile)
    def _(j):
        gate = jnp.dot(normed[...], wg[:, column(j)], preferred_element_type=F32)
        upper = jnp.dot(normed[...], wu[:, column(j)], preferred_element_type=F32)
        act[:, column(j)] = (gate * jax.nn.sigmoid(gate) * upper).astype(BF)

    loads[3].wait()
    steps = width // 2 // tile
    swaps = []
    for j in range(steps):
        cols = pl.ds(j * tile, tile)
        half_out[:, cols] = jnp.dot(
            act[...], wd[:, column((1 - t) * steps + j)], preferred_element_type=F32
        ).astype(BF)
        swap = push(half_out.at[:, cols], half_in.at[:, cols], sf.at[j], rf.at[j], tp=1 - t)
        swap.start()
        swaps.append(swap)
    for j in range(steps):
        cols = pl.ds(j * tile, tile)
        term = jnp.dot(act[...], wd[:, column(t * steps + j)], preferred_element_type=F32)
        swaps[j].wait()
        out = mid[:, column(t * steps + j)].astype(F32) + (term + half_in[:, cols].astype(F32))
        ready[:, :, cols] = out.astype(BF).reshape(n, rows // n, tile)
        if j % 2:
            c = j // 2
            both = pl.ds(c * 2 * tile, 2 * tile)
            copy = pltpu.make_async_copy(ready.at[me, :, both], arrived.at[me, :, both], local.at[2 + c])
            copy.start()
            late.append(copy)
            for k in range(1, n):
                there = lax.rem(me + k, n)
                copy = push(ready.at[there, :, both], arrived.at[me, :, both], sx.at[c, k - 1], rx.at[c, k - 1],
                            seq=there)
                copy.start()
                late.append(copy)
    for copy in late:
        copy.wait()


def finish(attn, xs, gain, cache, wo, wg, wu, wd, n):
    rows, width = xs.shape
    half, hidden = width // 2, wg.shape[1]
    dma = pltpu.SemaphoreType.DMA
    vmem = pl.BlockSpec(memory_space=pltpu.VMEM)
    anywhere = pl.BlockSpec(memory_space=pl.ANY)
    room = lambda *shape: pltpu.VMEM(shape, BF)
    return pl.pallas_call(
        lambda *refs: finish_kernel(n, *refs),
        in_specs=[anywhere, vmem, vmem] + [anywhere] * 5,
        out_specs=[anywhere] * 2,
        out_shape=[jax.ShapeDtypeStruct((n, rows // n, half), BF), jax.ShapeDtypeStruct(cache.shape, BF)],
        scratch_shapes=[room(*wo.shape), room(*wg.shape), room(*wu.shape), room(*wd.shape),
                        room(4, n, rows // n, 2 * HD),
                        room(rows, width), room(rows, width), room(rows, width), room(rows, width),
                        room(rows, hidden), room(rows, half), room(rows, half),
                        room(n, rows // n, half),
                        dma((4,)), dma((4,)), dma((3,)), dma((3,)), dma((4,)), dma((4,)), dma((4,)), dma((4,)),
                        dma((2, n - 1)), dma((2, n - 1)), dma((n - 1,)), dma((n - 1,))],
        compiler_params=pltpu.CompilerParams(
            collective_id=1, has_side_effects=True, vmem_limit_bytes=VMEM_BYTES
        ),
    )(attn, xs, gain, cache, wo, wg, wu, wd)


def unsort_kernel(landed_ref, target_ref, out_ref, cache_ref, hidden_ref, kv_ref):
    rows = out_ref.shape[0]
    row = lax.broadcasted_iota(jnp.int32, (rows, rows), 0)
    for index, source, result in ((landed_ref, out_ref, hidden_ref), (target_ref, cache_ref, kv_ref)):
        chosen = jnp.where(row == index[...], 1.0, 0.0).astype(BF)
        result[...] = jnp.dot(chosen, source[...], preferred_element_type=F32).astype(BF)


def unsort(landed, target, out, cache):
    rows, width = out.shape
    tile = 512
    index = pl.BlockSpec((1, rows), lambda j: (0, 0))
    block = pl.BlockSpec((rows, tile), lambda j: (0, j))
    return pl.pallas_call(
        unsort_kernel,
        grid=(width // tile,),
        in_specs=[index, index, block, block],
        out_specs=[block, block],
        out_shape=[jax.ShapeDtypeStruct(out.shape, BF), jax.ShapeDtypeStruct(cache.shape, BF)],
    )(landed, target, out, cache)


def fast_body(
    hidden_in, token_order, span_lengths, placement, norm_in, q_weight, k_weight, v_weight, q_gain, k_gain,
    o_weight, norm_mid, gate_weight, up_weight, down_weight,
):
    rows, width = hidden_in.shape
    n = lax.axis_size("seq")
    me = lax.axis_index("seq")
    share = BLK // n
    slot_rows = (placement[:, None] * share + jnp.arange(share, dtype=jnp.int32)[None, :]).reshape(rows)
    chosen = slot_rows[:, None] == jnp.arange(rows, dtype=jnp.int32)[None, :]
    order = jnp.sum(jnp.where(chosen, token_order[None, :], 0), axis=1)
    pos = order - request_start(order, span_lengths)
    half = HD // 2
    freq = THETA ** (-jnp.arange(half, dtype=F32) * 2.0 / HD)
    lane = jnp.arange(HD)
    angle = pos.astype(F32)[:, None] * jnp.tile(freq, 2)[None, :]
    cosine = jnp.cos(angle)
    sine = jnp.sin(angle) * jnp.where(lane < half, -1.0, 1.0)[None, :]
    xs, q, kv, stacked = project(
        hidden_in, chosen.astype(BF), norm_in[None, :], cosine, sine, q_gain[None, :], k_gain[None, :],
        q_weight, k_weight, v_weight,
    )
    group = rows // n
    split = lambda a: a.reshape(a.shape[0], n, group, a.shape[2])
    orders = jnp.concatenate(
        [order[None, :], token_order[None, :], jnp.zeros((6, rows), jnp.int32)], axis=0
    )
    kv_all, q_all, orders_all = exchange(split(kv), split(q), orders, n)
    by_pair = orders_all[:, 0, :].reshape(n, n, group)
    keys = by_pair.transpose(1, 0, 2).reshape(n // 2, 2 * n * group)
    mine = lax.dynamic_index_in_dim(by_pair.reshape(4, 4, n, group), lax.rem(me, 4), 1, keepdims=False)
    token = mine.transpose(1, 0, 2).reshape(n * 4 * group)
    info = jnp.stack([token, request_start(token, span_lengths)], axis=1)
    low = request_start(jnp.arange(n // 2, dtype=jnp.int32) * (2 * rows), span_lengths) // (2 * rows)
    attn = attend(low, q_all, kv_all, info, keys)
    row_ids = jnp.arange(rows, dtype=jnp.int32)
    landed = lax.dynamic_index_in_dim(by_pair, me, 1, keepdims=False).reshape(rows) - me * rows
    anchor = lax.dynamic_index_in_dim(
        orders_all[:, 1, :].reshape(n, n, group), me, 1, keepdims=False
    ).reshape(rows)
    target = row_ids % group // share * BLK + anchor % BLK
    cache_width = stacked.shape[1]
    arrived, cache_all = finish(
        attn, xs, norm_mid[None, :], stacked.reshape(n, group, cache_width),
        o_weight, gate_weight, up_weight, down_weight, n
    )
    hidden_out, kv_cache = unsort(
        landed[None, :], target[None, :], arrived.reshape(rows, width // 2), cache_all.reshape(rows, cache_width)
    )
    kv_cache = kv_cache.reshape(rows // BLK, BLK, cache_width)
    return (hidden_out, kv_cache)


def solution(mesh):
    in_specs = (
        P("seq", None),
        P("seq"),
        P(),
        P(),
        P(),
        P(None, "tp"),
        P(None, "tp"),
        P(None, "tp"),
        P(),
        P(),
        P("tp", None),
        P(),
        P(None, "tp"),
        P(None, "tp"),
        P("tp", None),
    )
    out_specs = (P("seq", "tp"), P("seq", None, "tp"))
    chosen = fast_body if mesh.shape["seq"] == 16 and mesh.shape["tp"] == 2 else body
    return jax.shard_map(chosen, mesh=mesh, in_specs=in_specs, out_specs=out_specs, check_vma=False)
```

```python
import jax
import jax.numpy as jnp
from jax import lax
from jax.experimental import pallas as pl
from jax.experimental.pallas import tpu as pltpu
from jax.sharding import PartitionSpec as P

HD = 128
BLK = 128


EPS = 1e-06
THETA = 1000000.0


def rms(values, gain):
    return values * lax.rsqrt(jnp.mean(values * values, axis=-1, keepdims=True) + EPS) * gain


def rotary(values, pos):
    half = values.shape[-1] // 2
    freq = THETA ** (-jnp.arange(half, dtype=jnp.float32) * 2.0 / values.shape[-1])
    angle = pos.astype(jnp.float32)[:, None] * freq[None, :]
    cosine = jnp.cos(angle)[:, None, :]
    sine = jnp.sin(angle)[:, None, :]
    first = values[..., :half]
    second = values[..., half:]
    return jnp.concatenate(
        [first * cosine - second * sine, second * cosine + first * sine], axis=-1
    )


def request_start(order, lengths):
    index = jnp.arange(lengths.shape[0])
    begins = jnp.sum(jnp.where(index[None, :] < index[:, None], lengths[None, :], 0), axis=1)
    return jnp.max(jnp.where(begins[None, :] <= order[:, None], begins[None, :], 0), axis=1)


def relay_cache(stacked, token_order, rows, seq_count):
    arrived, anchor = (
        lax.all_to_all(stacked, "seq", split_axis=0, concat_axis=0, tiled=True),
        lax.all_to_all(token_order, "seq", split_axis=0, concat_axis=0, tiled=True),
    )
    group_rows = rows // seq_count
    share = BLK // seq_count
    local_slot = jnp.arange(rows, dtype=jnp.int32) % group_rows // share
    target = local_slot * BLK + anchor % BLK
    cache = jnp.zeros(stacked.shape, jnp.bfloat16).at[target].set(arrived)
    return cache.reshape(rows // BLK, BLK, stacked.shape[1])


def body(
    hidden_in,
    token_order,
    span_lengths,
    placement,
    norm_in,
    q_weight,
    k_weight,
    v_weight,
    q_gain,
    k_gain,
    o_weight,
    norm_mid,
    gate_weight,
    up_weight,
    down_weight,
):
    rows, width = hidden_in.shape
    seq_count = lax.axis_size("seq")
    tp_count = lax.axis_size("tp")
    part = width // tp_count
    kv_heads = k_weight.shape[1] // HD
    q_heads = q_weight.shape[1] // HD
    group = q_heads // kv_heads
    xfull = hidden_in.astype(jnp.float32)
    normed = rms(xfull, norm_in).astype(jnp.bfloat16)
    begin = request_start(token_order, span_lengths)
    pos = token_order - begin
    query = jnp.dot(normed, q_weight, preferred_element_type=jnp.float32).reshape(rows, q_heads, HD)
    keys = jnp.dot(normed, k_weight, preferred_element_type=jnp.float32).reshape(rows, kv_heads, HD)
    values = (
        jnp.dot(normed, v_weight, preferred_element_type=jnp.float32)
        .reshape(rows, kv_heads, HD)
        .astype(jnp.bfloat16)
    )
    qnorm = rotary(rms(query, q_gain), pos).astype(jnp.bfloat16).reshape(rows, kv_heads, group, HD)
    knorm = rotary(rms(keys, k_gain), pos).astype(jnp.bfloat16)
    stacked = jnp.stack([knorm, values], axis=2).reshape(rows, kv_heads * 2 * HD)
    scale = 1.0 / HD**0.5
    start_best = jnp.full((rows, kv_heads, group), -1e30, jnp.float32)
    best = start_best
    piece_keys = lax.all_gather(knorm, "seq", axis=0, tiled=True)
    piece_values = lax.all_gather(values, "seq", axis=0, tiled=True)
    piece_order = lax.all_gather(token_order, "seq", axis=0, tiled=True)
    score = (
        jnp.einsum("qkge,nke->qkgn", qnorm, piece_keys, preferred_element_type=jnp.float32) * scale
    )
    mask = (piece_order[None, :] >= begin[:, None]) & (piece_order[None, :] <= token_order[:, None])
    mask = mask[:, None, None, :]
    score = jnp.where(mask, score, -1e30)
    new_best = jnp.maximum(best, jnp.max(score, axis=-1))
    weights = jnp.where(mask, jnp.exp(score - new_best[..., None]), 0.0)
    total = jnp.sum(weights, axis=-1)
    accum = jnp.einsum(
        "qkgn,nke->qkge",
        weights.astype(jnp.bfloat16),
        piece_values,
        preferred_element_type=jnp.float32,
    )
    best, total, accum = (new_best, total, accum)
    attn = (accum / total[..., None]).astype(jnp.bfloat16).reshape(rows, q_heads * HD)
    terms = jnp.dot(attn, o_weight, preferred_element_type=jnp.float32)
    column = lax.axis_index("tp") * part
    own_input = lax.dynamic_slice_in_dim(xfull, column, part, 1)
    mid = (
        own_input
        + lax.psum_scatter(
            terms.astype(jnp.bfloat16), "tp", scatter_dimension=1, tiled=True
        ).astype(jnp.float32)
    ).astype(jnp.bfloat16)
    mid_full = lax.all_gather(mid, "tp", axis=1, tiled=True)
    normed_mid = rms(mid_full.astype(jnp.float32), norm_mid).astype(jnp.bfloat16)
    gate = jnp.dot(normed_mid, gate_weight, preferred_element_type=jnp.float32)
    upper = jnp.dot(normed_mid, up_weight, preferred_element_type=jnp.float32)
    act = (jax.nn.silu(gate) * upper).astype(jnp.bfloat16)
    feed = lax.psum_scatter(
        jnp.dot(act, down_weight, preferred_element_type=jnp.float32).astype(jnp.bfloat16),
        "tp",
        scatter_dimension=1,
        tiled=True,
    ).astype(jnp.float32)
    out = (mid.astype(jnp.float32) + feed).astype(jnp.bfloat16)
    blocks_dev = rows // BLK
    share = BLK // seq_count
    slots = placement.reshape(seq_count, blocks_dev)
    send_rows = (
        slots[:, :, None] * share + jnp.arange(share, dtype=jnp.int32)[None, None, :]
    ).reshape(rows)
    arrived, anchor = (
        lax.all_to_all(out[send_rows], "seq", split_axis=0, concat_axis=0, tiled=True),
        lax.all_to_all(token_order[send_rows], "seq", split_axis=0, concat_axis=0, tiled=True),
    )
    local_row = anchor - lax.axis_index("seq") * rows
    hidden_out = jnp.zeros_like(out).at[local_row].set(arrived)
    kv_cache = relay_cache(stacked, token_order, rows, seq_count)
    return (hidden_out, kv_cache)


BF = jnp.bfloat16
F32 = jnp.float32
VMEM_BYTES = 56 * 1024 * 1024


def project_kernel(x_ref, sel_ref, gain_ref, cos_ref, sin_ref, qg_ref, kg_ref, qw_ref, kw_ref, vw_ref,
                   xs_ref, q_ref, kv_ref, stacked_ref, normed):
    @pl.when(pl.program_id(0) == 0)
    def _():
        xs = jnp.dot(sel_ref[...], x_ref[...], preferred_element_type=F32)
        xs_ref[...] = xs.astype(BF)
        normed[...] = (
            xs * lax.rsqrt(jnp.mean(xs * xs, axis=-1, keepdims=True) + EPS) * gain_ref[...]
        ).astype(BF)

    cosine, sine = cos_ref[...], sin_ref[...]

    def turned(u, gain):
        u = u * lax.rsqrt(jnp.mean(u * u, axis=-1, keepdims=True) + EPS) * gain
        return (u * cosine + pltpu.roll(u, HD // 2, 1) * sine).astype(BF)

    base = normed[...]
    q = jnp.dot(base, qw_ref[...], preferred_element_type=F32)
    q_ref[0, :, :HD] = turned(q[:, :HD], qg_ref[...])
    q_ref[0, :, HD:] = turned(q[:, HD:], qg_ref[...])
    k = turned(jnp.dot(base, kw_ref[...], preferred_element_type=F32), kg_ref[...])
    v = jnp.dot(base, vw_ref[...], preferred_element_type=F32).astype(BF)
    kv = jnp.concatenate([k, v], axis=1)
    kv_ref[0] = kv
    stacked_ref[...] = lax.dot_general(
        sel_ref[...], kv, (((0,), (0,)), ((), ())), preferred_element_type=F32
    ).astype(BF)


def project(x, sel, gain, cosine, sine, qg, kg, qw, kw, vw):
    rows, width = x.shape
    heads = kw.shape[1] // HD
    whole = lambda shape: pl.BlockSpec(shape, lambda h: (0, 0))
    column = lambda cols: pl.BlockSpec((width, cols), lambda h: (0, h))
    head = pl.BlockSpec((1, rows, 2 * HD), lambda h: (h, 0, 0))
    return pl.pallas_call(
        project_kernel,
        grid=(heads,),
        in_specs=[whole((rows, width)), whole((rows, rows)), whole((1, width)), whole((rows, HD)),
                  whole((rows, HD)), whole((1, HD)), whole((1, HD)), column(2 * HD), column(HD), column(HD)],
        out_specs=[whole((rows, width)), head, head, pl.BlockSpec((rows, 2 * HD), lambda h: (0, h))],
        out_shape=[jax.ShapeDtypeStruct((rows, width), BF),
                   jax.ShapeDtypeStruct((heads, rows, 2 * HD), BF),
                   jax.ShapeDtypeStruct((heads, rows, 2 * HD), BF),
                   jax.ShapeDtypeStruct((rows, heads * 2 * HD), BF)],
        scratch_shapes=[pltpu.VMEM((rows, width), BF)],
        compiler_params=pltpu.CompilerParams(vmem_limit_bytes=VMEM_BYTES),
    )(x, sel, gain, cosine, sine, qg, kg, qw, kw, vw)


def greet(seq_count, sibling):
    barrier = pltpu.get_barrier_semaphore()
    me = lax.axis_index("seq")
    for k in range(1, seq_count):
        pl.semaphore_signal(barrier, inc=1, device_id={"seq": lax.rem(me + k, seq_count)})
    if sibling:
        pl.semaphore_signal(barrier, inc=1, device_id={"tp": 1 - lax.axis_index("tp")})
    pl.semaphore_wait(barrier, seq_count - 1 + (1 if sibling else 0))


def push(src, dst, send, recv, **where):
    return pltpu.make_async_remote_copy(
        src_ref=src, dst_ref=dst, send_sem=send, recv_sem=recv, device_id=where
    )


def exchange_kernel(n, kv_ref, q_ref, order_ref, kv_out, q_out, order_out,
                    local, s1, r1, s2, r2, sq, rq, so, ro):
    me = lax.axis_index("seq")
    z, p = me // 4, lax.rem(me, 4)
    part = lambda seq: pl.ds(pl.multiple_of(seq * 16, 16), 16)
    own = [
        pltpu.make_async_copy(kv_ref.at[z], kv_out.at[:, part(me), :], local.at[0]),
        pltpu.make_async_copy(q_ref.at[z], q_out.at[:, part(z), :], local.at[1]),
        pltpu.make_async_copy(order_ref, order_out.at[me], local.at[2]),
    ]
    for copy in own:
        copy.start()
    greet(n, False)
    first, second, query, orders = [], [], [], []
    for d in (1, 2, 3):
        there = lax.rem(z + d, 4)
        copy = push(kv_ref.at[there], kv_out.at[:, part(me), :], s1.at[d - 1], r1.at[d - 1], seq=there * 4 + p)
        copy.start()
        first.append(copy)
    for k in (1, 2, 3):
        copy = push(kv_ref.at[z], kv_out.at[:, part(me), :], s2.at[0, k - 1], r2.at[0, k - 1],
                    seq=z * 4 + lax.rem(p + k, 4))
        copy.start()
        second.append(copy)
    for k in range(1, n):
        copy = push(order_ref, order_out.at[me], so.at[k - 1], ro.at[k - 1], seq=lax.rem(me + k, n))
        copy.start()
        orders.append(copy)
    for d in (1, 2, 3):
        there = lax.rem(z + d, 4)
        copy = push(q_ref.at[there], q_out.at[:, part(z), :], sq.at[d - 1], rq.at[d - 1], seq=there * 4 + p)
        copy.start()
        query.append(copy)
    for d in (1, 3, 2):
        first[d - 1].wait_recv()
        rows = part(lax.rem(z + 4 - d, 4) * 4 + p)
        for k in (1, 2, 3):
            copy = push(kv_out.at[:, rows, :], kv_out.at[:, rows, :], s2.at[d, k - 1], r2.at[d, k - 1],
                        seq=z * 4 + lax.rem(p + k, 4))
            copy.start()
            second.append(copy)
    for copy in own:
        copy.wait()
    for copy in first:
        copy.wait_send()
    for copy in second + query + orders:
        copy.wait()


def exchange(kv, q, orders, n):
    heads = kv.shape[0]
    dma = pltpu.SemaphoreType.DMA
    anywhere = pl.BlockSpec(memory_space=pl.ANY)
    width = kv.shape[-1]
    return pl.pallas_call(
        lambda *refs: exchange_kernel(n, *refs),
        in_specs=[anywhere] * 3,
        out_specs=[anywhere] * 3,
        out_shape=[jax.ShapeDtypeStruct((n, n * 16, width), BF),
                   jax.ShapeDtypeStruct((n, 4 * 16, width), BF),
                   jax.ShapeDtypeStruct((n,) + orders.shape, jnp.int32)],
        scratch_shapes=[dma((3,)), dma((3,)), dma((3,)), dma((4, 3)), dma((4, 3)), dma((3,)), dma((3,)),
                        dma((n - 1,)), dma((n - 1,))],
        compiler_params=pltpu.CompilerParams(collective_id=0, has_side_effects=True),
    )(kv, q, orders)


def attend_kernel(low_ref, q_ref, kv_ref, info_ref, key_ref, out_ref):
    i = pl.program_id(0)
    q = q_ref[...].reshape(128, 2 * HD)
    both = jnp.concatenate([q[:, :HD], q[:, HD:]], axis=0)
    token, begin = info_ref[:, 0:1], info_ref[:, 1:2]
    scale = 1.0 / HD**0.5

    key_all = key_ref[...]
    which = lax.broadcasted_iota(jnp.int32, key_all.shape, 0)

    def step(j, carry):
        best, total, accum = carry
        kv = kv_ref[pl.ds(2 * j, 2)].reshape(512, 2 * HD)
        score = lax.dot_general(
            both, kv[:, :HD], (((1,), (1,)), ((), ())), preferred_element_type=F32
        ) * scale
        keys = jnp.sum(jnp.where(which == j, key_all, 0), axis=0, keepdims=True)
        mask = (keys >= begin) & (keys <= token)
        score = jnp.where(jnp.concatenate([mask, mask], axis=0), score, -1e30)
        new_best = jnp.maximum(best, jnp.max(score, axis=1, keepdims=True))
        weights = jnp.exp(score - new_best)
        shrink = jnp.exp(best - new_best)
        total = total * shrink + jnp.sum(weights, axis=1, keepdims=True)
        accum = accum * shrink + jnp.dot(weights.astype(BF), kv[:, HD:], preferred_element_type=F32)
        return new_best, total, accum

    start = (jnp.full((256, 1), -1e30, F32), jnp.zeros((256, 1), F32), jnp.zeros((256, HD), F32))
    _, total, accum = lax.fori_loop(low_ref[i], i + 1, step, start)
    attn = (accum / total).astype(BF)
    out_ref[...] = jnp.concatenate([attn[:128], attn[128:]], axis=1).reshape(2, 64, 2 * HD)


def attend(low, q, kv, info, keys):
    tiles = q.shape[0] // 2
    block = pl.BlockSpec((2, 64, 2 * HD), lambda i, low: (i, 0, 0))
    return pl.pallas_call(
        attend_kernel,
        grid_spec=pltpu.PrefetchScalarGridSpec(
            num_scalar_prefetch=1,
            grid=(tiles,),
            in_specs=[block, pl.BlockSpec(kv.shape, lambda i, low: (0, 0, 0)),
                      pl.BlockSpec((128, 2), lambda i, low: (i, 0)),
                      pl.BlockSpec(keys.shape, lambda i, low: (0, 0))],
            out_specs=block,
        ),
        out_shape=jax.ShapeDtypeStruct(q.shape, BF),
        compiler_params=pltpu.CompilerParams(vmem_limit_bytes=VMEM_BYTES),
    )(low, q, kv, info, keys)


def finish_kernel(n, attn_ref, xs_ref, gain_ref, cache_ref, wo_hbm, wg_hbm, wu_hbm, wd_hbm, arrived, cache_out,
                  wo, wg, wu, wd, attn, sent, came, mid, normed, act, half_out, half_in, ready,
                  wsem, local, sa, ra, st, rt, sf, rf, sx, rx, sc, rc):
    me, t = lax.axis_index("seq"), lax.axis_index("tp")
    z, p = me // 4, lax.rem(me, 4)
    part = lambda seq: pl.ds(pl.multiple_of(seq * 16, 16), 16)
    loads = [pltpu.make_async_copy(a, b, wsem.at[i])
             for i, (a, b) in enumerate(((wo_hbm, wo), (wg_hbm, wg), (wu_hbm, wu), (wd_hbm, wd)))]
    for load in loads:
        load.start()
    keep = pltpu.make_async_copy(attn_ref.at[:, part(z), :], attn.at[z], local.at[0])
    keep.start()
    late = [pltpu.make_async_copy(cache_ref.at[me], cache_out.at[me], local.at[1])]
    late[0].start()
    greet(n, True)
    moves = []
    for d in (1, 2, 3):
        there = lax.rem(z + d, 4)
        copy = push(attn_ref.at[:, part(there), :], attn.at[z], sa.at[d - 1], ra.at[d - 1], seq=there * 4 + p)
        copy.start()
        moves.append(copy)
    loads[0].wait()
    keep.wait()
    for copy in moves:
        copy.wait()
    for k in range(1, n):
        there = lax.rem(me + k, n)
        copy = push(cache_ref.at[there], cache_out.at[me], sc.at[k - 1], rc.at[k - 1], seq=there)
        copy.start()
        late.append(copy)
    rows, width = xs_ref.shape
    tile = 256
    column = lambda j: pl.ds(pl.multiple_of(j * tile, tile), tile)
    swaps = []
    for j in range(width // tile):
        result = jnp.zeros((rows, tile), F32)
        for h in range(4):
            result += jnp.dot(attn[h].reshape(rows, 2 * HD), wo[h * 256:(h + 1) * 256, j * tile:(j + 1) * tile],
                              preferred_element_type=F32)
        sent[:, j * tile:(j + 1) * tile] = result.astype(BF)
        if j % 2:
            c = j // 2
            both = pl.ds(c * 2 * tile, 2 * tile)
            swap = push(sent.at[:, both], came.at[:, both], st.at[c], rt.at[c], tp=1 - t)
            swap.start()
            swaps.append(swap)
    square = jnp.zeros((rows, 1), F32)
    for c, swap in enumerate(swaps):
        swap.wait()
        cols = slice(c * 2 * tile, (c + 1) * 2 * tile)
        piece = xs_ref[:, cols].astype(F32) + (sent[:, cols].astype(F32) + came[:, cols].astype(F32))
        piece = piece.astype(BF)
        mid[:, cols] = piece
        piece = piece.astype(F32)
        square += jnp.sum(piece * piece, axis=-1, keepdims=True)
    factor = lax.rsqrt(square / width + EPS)
    for c in range(len(swaps)):
        cols = slice(c * 2 * tile, (c + 1) * 2 * tile)
        normed[:, cols] = (mid[:, cols].astype(F32) * factor * gain_ref[:, cols]).astype(BF)
    loads[1].wait()
    loads[2].wait()

    @pl.loop(0, act.shape[1] // tile)
    def _(j):
        gate = jnp.dot(normed[...], wg[:, column(j)], preferred_element_type=F32)
        upper = jnp.dot(normed[...], wu[:, column(j)], preferred_element_type=F32)
        act[:, column(j)] = (gate * jax.nn.sigmoid(gate) * upper).astype(BF)

    loads[3].wait()
    steps = width // 2 // tile
    swaps = []
    for j in range(steps):
        cols = pl.ds(j * tile, tile)
        half_out[:, cols] = jnp.dot(
            act[...], wd[:, column((1 - t) * steps + j)], preferred_element_type=F32
        ).astype(BF)
        swap = push(half_out.at[:, cols], half_in.at[:, cols], sf.at[j], rf.at[j], tp=1 - t)
        swap.start()
        swaps.append(swap)
    for j in range(steps):
        cols = pl.ds(j * tile, tile)
        term = jnp.dot(act[...], wd[:, column(t * steps + j)], preferred_element_type=F32)
        swaps[j].wait()
        out = mid[:, column(t * steps + j)].astype(F32) + (term + half_in[:, cols].astype(F32))
        ready[:, :, cols] = out.astype(BF).reshape(n, rows // n, tile)
        if j % 2:
            c = j // 2
            both = pl.ds(c * 2 * tile, 2 * tile)
            copy = pltpu.make_async_copy(ready.at[me, :, both], arrived.at[me, :, both], local.at[2 + c])
            copy.start()
            late.append(copy)
            for k in range(1, n):
                there = lax.rem(me + k, n)
                copy = push(ready.at[there, :, both], arrived.at[me, :, both], sx.at[c, k - 1], rx.at[c, k - 1],
                            seq=there)
                copy.start()
                late.append(copy)
    for copy in late:
        copy.wait()


def finish(attn, xs, gain, cache, wo, wg, wu, wd, n):
    rows, width = xs.shape
    half, hidden = width // 2, wg.shape[1]
    dma = pltpu.SemaphoreType.DMA
    vmem = pl.BlockSpec(memory_space=pltpu.VMEM)
    anywhere = pl.BlockSpec(memory_space=pl.ANY)
    room = lambda *shape: pltpu.VMEM(shape, BF)
    return pl.pallas_call(
        lambda *refs: finish_kernel(n, *refs),
        in_specs=[anywhere, vmem, vmem] + [anywhere] * 5,
        out_specs=[anywhere] * 2,
        out_shape=[jax.ShapeDtypeStruct((n, rows // n, half), BF), jax.ShapeDtypeStruct(cache.shape, BF)],
        scratch_shapes=[room(*wo.shape), room(*wg.shape), room(*wu.shape), room(*wd.shape),
                        room(4, n, rows // n, 2 * HD),
                        room(rows, width), room(rows, width), room(rows, width), room(rows, width),
                        room(rows, hidden), room(rows, half), room(rows, half),
                        room(n, rows // n, half),
                        dma((4,)), dma((4,)), dma((3,)), dma((3,)), dma((4,)), dma((4,)), dma((4,)), dma((4,)),
                        dma((2, n - 1)), dma((2, n - 1)), dma((n - 1,)), dma((n - 1,))],
        compiler_params=pltpu.CompilerParams(
            collective_id=1, has_side_effects=True, vmem_limit_bytes=VMEM_BYTES
        ),
    )(attn, xs, gain, cache, wo, wg, wu, wd)


def unsort_kernel(landed_ref, target_ref, out_ref, cache_ref, hidden_ref, kv_ref):
    rows = out_ref.shape[0]
    row = lax.broadcasted_iota(jnp.int32, (rows, rows), 0)
    for index, source, result in ((landed_ref, out_ref, hidden_ref), (target_ref, cache_ref, kv_ref)):
        chosen = jnp.where(row == index[...], 1.0, 0.0).astype(BF)
        result[...] = jnp.dot(chosen, source[...], preferred_element_type=F32).astype(BF)


def unsort(landed, target, out, cache):
    rows, width = out.shape
    tile = 512
    index = pl.BlockSpec((1, rows), lambda j: (0, 0))
    block = pl.BlockSpec((rows, tile), lambda j: (0, j))
    return pl.pallas_call(
        unsort_kernel,
        grid=(width // tile,),
        in_specs=[index, index, block, block],
        out_specs=[block, block],
        out_shape=[jax.ShapeDtypeStruct(out.shape, BF), jax.ShapeDtypeStruct(cache.shape, BF)],
    )(landed, target, out, cache)


def fast_body(
    hidden_in, token_order, span_lengths, placement, norm_in, q_weight, k_weight, v_weight, q_gain, k_gain,
    o_weight, norm_mid, gate_weight, up_weight, down_weight,
):
    rows, width = hidden_in.shape
    n = lax.axis_size("seq")
    me = lax.axis_index("seq")
    share = BLK // n
    slot_rows = (placement[:, None] * share + jnp.arange(share, dtype=jnp.int32)[None, :]).reshape(rows)
    chosen = slot_rows[:, None] == jnp.arange(rows, dtype=jnp.int32)[None, :]
    order = jnp.sum(jnp.where(chosen, token_order[None, :], 0), axis=1)
    pos = order - request_start(order, span_lengths)
    half = HD // 2
    freq = THETA ** (-jnp.arange(half, dtype=F32) * 2.0 / HD)
    lane = jnp.arange(HD)
    angle = pos.astype(F32)[:, None] * jnp.tile(freq, 2)[None, :]
    cosine = jnp.cos(angle)
    sine = jnp.sin(angle) * jnp.where(lane < half, -1.0, 1.0)[None, :]
    xs, q, kv, stacked = project(
        hidden_in, chosen.astype(BF), norm_in[None, :], cosine, sine, q_gain[None, :], k_gain[None, :],
        q_weight, k_weight, v_weight,
    )
    group = rows // n
    split = lambda a: a.reshape(a.shape[0], n, group, a.shape[2])
    orders = jnp.concatenate(
        [order[None, :], token_order[None, :], jnp.zeros((6, rows), jnp.int32)], axis=0
    )
    kv_all, q_all, orders_all = exchange(split(kv), split(q), orders, n)
    by_pair = orders_all[:, 0, :].reshape(n, n, group)
    keys = by_pair.transpose(1, 0, 2).reshape(n // 2, 2 * n * group)
    mine = lax.dynamic_index_in_dim(by_pair.reshape(4, 4, n, group), lax.rem(me, 4), 1, keepdims=False)
    token = mine.transpose(1, 0, 2).reshape(n * 4 * group)
    info = jnp.stack([token, request_start(token, span_lengths)], axis=1)
    low = request_start(jnp.arange(n // 2, dtype=jnp.int32) * (2 * rows), span_lengths) // (2 * rows)
    attn = attend(low, q_all, kv_all, info, keys)
    row_ids = jnp.arange(rows, dtype=jnp.int32)
    landed = lax.dynamic_index_in_dim(by_pair, me, 1, keepdims=False).reshape(rows) - me * rows
    anchor = lax.dynamic_index_in_dim(
        orders_all[:, 1, :].reshape(n, n, group), me, 1, keepdims=False
    ).reshape(rows)
    target = row_ids % group // share * BLK + anchor % BLK
    cache_width = stacked.shape[1]
    arrived, cache_all = finish(
        attn, xs, norm_mid[None, :], stacked.reshape(n, group, cache_width),
        o_weight, gate_weight, up_weight, down_weight, n
    )
    hidden_out, kv_cache = unsort(
        landed[None, :], target[None, :], arrived.reshape(rows, width // 2), cache_all.reshape(rows, cache_width)
    )
    kv_cache = kv_cache.reshape(rows // BLK, BLK, cache_width)
    return (hidden_out, kv_cache)


def solution(mesh):
    in_specs = (
        P("seq", None),
        P("seq"),
        P(),
        P(),
        P(),
        P(None, "tp"),
        P(None, "tp"),
        P(None, "tp"),
        P(),
        P(),
        P("tp", None),
        P(),
        P(None, "tp"),
        P(None, "tp"),
        P("tp", None),
    )
    out_specs = (P("seq", "tp"), P("seq", None, "tp"))
    chosen = fast_body if mesh.shape["seq"] == 16 and mesh.shape["tp"] == 2 else body
    return jax.shard_map(chosen, mesh=mesh, in_specs=in_specs, out_specs=out_specs, check_vma=False)
```
